256 devices in a mesh: ta: 4 (over z_lo), sa: 64 (over x, y, z_hi, core).
Axes of the slice: x: 4, y: 4, z: 8 (z_hi: 2, z_lo: 4; z = z_hi * 4 + z_lo), core: 2. Of those that a mesh axis runs over, the one named last changes fastest.
Arguments:
- video_q: bfloat16 [4, 64, 384, 1536], P('ta', 'sa'), may hold values from -8 to 8
- video_k: bfloat16 [4, 64, 384, 1536], P('ta', 'sa'), may hold values from -8 to 8
- video_v: bfloat16 [4, 64, 384, 1536], P('ta', 'sa'), may hold values from -6 to 6
- text_q: bfloat16 [256, 1536], P(('ta', 'sa')), may hold values from -8 to 8
- text_k: bfloat16 [256, 1536], P(('ta', 'sa')), may hold values from -8 to 8
- text_v: bfloat16 [256, 1536], P(('ta', 'sa')), may hold values from -6 to 6
- q_gain: float32 [128], replicated, may hold values from 1 to 5.5
- k_gain: float32 [128], replicated, may hold values from 1 to 5.5
- text_len: int32 [1], replicated, may hold values from 64 to 256
- window: int32 [12, 3], replicated, may hold values from 1 to 3, as said below
Outputs:
- video_out: bfloat16 [4, 64, 384, 1536], P('ta', 'sa')
- text_out: bfloat16 [256, 1536], P(('ta', 'sa'))
The draws below stay inside these ranges and needn't reach their ends.
Inputs may be any that keep to these rules, and one draw needn't show every extreme that they name: Each head's window is 1 or 3 tiles along each of time, spatial rows and spatial columns; exactly 2 heads have each of the windows (3,3,3), (1,3,3), (3,1,3), (3,3,1), (1,1,3) and (1,3,1).
All inputs are finite; a program needn't handle non-finite values.
Results may differ from the reference program's by a relative error of at most 0.018.
The reference program's roundings to bfloat16 on the way count: a program that leaves them out, or rounds other values in their place, can miss the bound.
Values may be sent and summed in bfloat16 or wider, within the bound.
A program may use at most 128 MiB of HBM per device.

```python
import math
import jax
import jax.numpy as jnp
import numpy as np
from jax import lax

HEADS = 12
HEAD_DIM = 128
SW = 8
TEXT = 256
TILE_TOK = 384
WIDTH = 1536
GROUP = 2
NT = 4
NS = 64
SH = 8


def video_base(key):
    return jax.random.normal(key, (NT, NS, TILE_TOK, WIDTH), jnp.float32)


def text_base(key):
    return jax.random.normal(jax.random.fold_in(key, 5), (TEXT, WIDTH), jnp.float32)


def draw_video_k(key, part):
    base = video_base(key)
    return base.astype(jnp.bfloat16)


def draw_video_q(key, part):
    base = video_base(key)
    key = jax.random.fold_in(key, 12)
    fresh = jax.random.normal(key, base.shape, jnp.float32)
    return fresh.astype(jnp.bfloat16)


def draw_text_k(key, part):
    base = text_base(key)
    return base.astype(jnp.bfloat16)


def draw_text_q(key, part):
    base = text_base(key)
    key = jax.random.fold_in(key, 14)
    fresh = jax.random.normal(key, base.shape, jnp.float32)
    return fresh.astype(jnp.bfloat16)


def gain_draw(key, lowest, highest):
    return jnp.exp(jax.random.uniform(key, (HEAD_DIM,), jnp.float32, math.log(lowest), math.log(highest)))


def draw_q_gain(key, part):
    key = jax.random.fold_in(key, 21)
    return gain_draw(key, 1.0, 2.5)


def draw_k_gain(key, part):
    key = jax.random.fold_in(key, 22)
    return gain_draw(key, 1.0, 2.5)


def draw_window(key, part):
    key = jax.random.fold_in(key, 31)
    order = jax.random.permutation(key, HEADS)
    shape_index = jnp.argsort(order) // GROUP
    table = jnp.array([[3, 3, 3], [1, 3, 3], [3, 1, 3], [3, 3, 1], [1, 1, 3], [1, 3, 1]], dtype=jnp.int32)
    picked = (shape_index[:, None] == jnp.arange(6, dtype=jnp.int32)[None, :]).astype(jnp.int32)
    return jnp.sum(picked[:, :, None] * table[None, :, :], axis=1).astype(jnp.int32)


def block_levels(rng, shape, cuts, low, top_value):
    level = 1.0
    for axis_at, parts in cuts:
        draws = jax.random.uniform(jax.random.fold_in(jax.random.fold_in(rng, 6), axis_at), (parts,), jnp.float32, low / len(cuts), top_value / len(cuts))
        level = level * jnp.repeat(jnp.exp(draws), shape[axis_at] // parts).reshape((-1,) + (1,) * (len(shape) - 1 - axis_at))
    return level


def normal_values(rng, shape, scale, reach, shards=(), held_as=jnp.bfloat16):
    values = jax.random.normal(rng, shape, jnp.float32) * scale
    if len(shards) > 0:
        values = block_levels(rng, shape, shards, -0.22, 0.18) * values
    return jnp.clip(values, min=-reach, max=reach).astype(held_as)


def setup_inputs(seed: int = 0) -> dict:
    keys = jax.random.split(jax.random.key(seed), 11)
    return {
        "video_q": draw_video_q(jax.random.fold_in(keys[10], 71), 0),
        "video_k": draw_video_k(jax.random.fold_in(keys[10], 71), 0),
        "video_v": normal_values(keys[2], (NT, NS, TILE_TOK, WIDTH), 1.0, 6.0, ((0, 4), (1, 64))),
        "text_q": draw_text_q(jax.random.fold_in(keys[10], 71), 0),
        "text_k": draw_text_k(jax.random.fold_in(keys[10], 71), 0),
        "text_v": normal_values(keys[5], (TEXT, WIDTH), 1.0, 6.0, ((0, 256),)),
        "q_gain": draw_q_gain(jax.random.fold_in(keys[10], 71), 0),
        "k_gain": draw_k_gain(jax.random.fold_in(keys[10], 71), 0),
        "text_len": jax.random.randint(keys[8], (1,), TEXT // 4, TEXT + 1).astype(jnp.int32),
        "window": draw_window(jax.random.fold_in(keys[10], 71), 0),
    }


EPSILON = 1e-06

def normalize(values, gain_vector):
    per_head = gain_vector.shape[0]
    shaped = values.astype(jnp.float32).reshape(values.shape[:-1] + (values.shape[-1] // per_head, per_head))
    spread = jnp.sqrt(lax.optimization_barrier(jnp.mean(shaped * shaped, axis=-1, keepdims=True)) + EPSILON)
    return (shaped / spread * gain_vector).astype(jnp.bfloat16)

def block_terms(queries, key_rows, value_rows, allowed, score_scale):
    scores = jnp.einsum('qhd,khd->hqk', queries.astype(jnp.float32), key_rows.astype(jnp.float32)) * score_scale
    scores = jnp.where(allowed, scores, -jnp.inf)
    highest = lax.optimization_barrier(jnp.max(scores, axis=-1))
    weights = jnp.exp(scores - highest[..., None])
    weight_total = lax.optimization_barrier(jnp.sum(weights, axis=-1))
    rounded = lax.optimization_barrier(weights.astype(jnp.bfloat16)).astype(jnp.float32)
    summed = jnp.einsum('hqk,khd->hqd', rounded, value_rows.astype(jnp.float32))
    return (highest, weight_total, summed)

def combine(earlier, later):
    joint_peak = jnp.maximum(earlier[0], later[0])
    early_factor = jnp.exp(earlier[0] - joint_peak)
    late_factor = jnp.exp(later[0] - joint_peak)
    return (joint_peak, earlier[1] * early_factor + later[1] * late_factor, earlier[2] * early_factor[..., None] + later[2] * late_factor[..., None])

def reference(video_q, video_k, video_v, text_q, text_k, text_v, q_gain, k_gain, text_len, window):
    head_count = window.shape[0]
    per_head = q_gain.shape[0]
    score_scale = 1.0 / math.sqrt(per_head)
    queries = normalize(video_q, q_gain)
    key_grid = normalize(video_k, k_gain)
    value_grid = video_v.reshape(key_grid.shape)
    text_queries = normalize(text_q, q_gain)
    text_keys = normalize(text_k, k_gain)
    text_values = text_v.reshape(text_keys.shape)
    tile_shape = (NT, SH, SW, TILE_TOK, head_count, per_head)
    margin = ((1, 1), (1, 1), (1, 1), (0, 0), (0, 0), (0, 0))
    padded_keys = jnp.pad(key_grid.reshape(tile_shape), margin)
    padded_values = jnp.pad(value_grid.reshape(tile_shape), margin)
    flat_queries = queries.reshape(NT * NS, TILE_TOK, head_count, per_head)
    offset_rows = np.array([[first - 1, second - 1, third - 1] for first in range(3) for second in range(3) for third in range(3)], dtype=np.int32)
    offset_table = jnp.asarray(offset_rows, dtype=jnp.int32)
    half_width = (window - 1) // 2
    head_sees = jnp.all(jnp.abs(offset_table)[None, :, :] <= half_width[:, None, :], axis=2)
    grid_limits = jnp.array([NT, SH, SW], dtype=jnp.int32)
    text_ok = jnp.arange(TEXT, dtype=jnp.int32) < text_len[0]
    text_allowed = jnp.broadcast_to(text_ok[None, :], (head_count, TEXT))

    def tile_out(tile_index):
        tile_index = tile_index.astype(jnp.int32)
        time_pos = (tile_index // NS).astype(jnp.int32)
        space_pos = (tile_index % NS).astype(jnp.int32)
        row_pos = (space_pos // SW).astype(jnp.int32)
        column_pos = (space_pos % SW).astype(jnp.int32)
        position = jnp.stack([time_pos, row_pos, column_pos]).astype(jnp.int32)
        shifted = position[None, :] + offset_table
        inside = jnp.all((shifted >= 0) & (shifted < grid_limits[None, :]), axis=1)
        zero_index = jnp.zeros((), jnp.int32)
        start = (time_pos, row_pos, column_pos, zero_index, zero_index, zero_index)
        extent = (3, 3, 3, TILE_TOK, head_count, per_head)
        near_keys = lax.dynamic_slice(padded_keys, start, extent).reshape(27 * TILE_TOK, head_count, per_head)
        near_values = lax.dynamic_slice(padded_values, start, extent).reshape(27 * TILE_TOK, head_count, per_head)
        video_allowed = jnp.repeat(head_sees & inside[None, :], TILE_TOK, axis=1)
        allowed = jnp.concatenate([video_allowed, text_allowed], axis=1)
        key_rows = jnp.concatenate([near_keys, text_keys], axis=0)
        value_rows = jnp.concatenate([near_values, text_values], axis=0)
        highest, weight_total, summed = block_terms(flat_queries[tile_index], key_rows, value_rows, allowed[:, None, :], score_scale)
        result = summed / weight_total[..., None]
        return jnp.transpose(result, (1, 0, 2)).reshape(TILE_TOK, head_count * per_head).astype(jnp.bfloat16)
    video_out = lax.map(tile_out, jnp.arange(NT * NS, dtype=jnp.int32)).reshape(NT, NS, TILE_TOK, head_count * per_head)
    flat_keys = key_grid.reshape(NT * NS, TILE_TOK, head_count, per_head)
    flat_values = value_grid.reshape(NT * NS, TILE_TOK, head_count, per_head)
    start_terms = block_terms(text_queries, text_keys, text_values, text_ok[None, None, :], score_scale)
    every_key = jnp.ones((TILE_TOK,), bool)

    def absorb(carry, tile_pair):
        terms = block_terms(text_queries, tile_pair[0], tile_pair[1], every_key[None, None, :], score_scale)
        return (combine(carry, terms), None)
    final_terms, unused = lax.scan(absorb, start_terms, (flat_keys, flat_values))
    text_result = final_terms[2] / final_terms[1][..., None]
    text_out = jnp.transpose(text_result, (1, 0, 2)).reshape(TEXT, head_count * per_head).astype(jnp.bfloat16)
    return (video_out, text_out)
```

```python
import functools
import math

import jax
import jax.numpy as jnp
from jax import lax
from jax.experimental import pallas as pl
from jax.experimental.pallas import tpu as pltpu
from jax.sharding import PartitionSpec as P

MESH = pl.DeviceIdType.MESH
EPS = 1e-6
F32, BF16 = jnp.float32, jnp.bfloat16
HEADS, D, TOK, TEXT = 12, 128, 384, 256
SW = 8
BIG = 1e30
TROWS = 48
VMEM_LIMIT = 61 * 2**20
RANK_OF_CODE = (0, 0, 5, 1, 0, 3, 4, 2)


def pre_kernel(order, vq, vk, vv, tq, tk, tv, qg, kg, q_out, kv_out, t_out, rows):
    i = pl.program_id(0)

    def norm(value, gain):
        u = value.astype(F32)
        spread = jnp.sqrt(jnp.mean(u * u, axis=-1, keepdims=True) + EPS)
        return u / spread * gain

    @pl.when(i == 0)
    def _():
        rows[...] = jnp.zeros_like(rows)

    q_out[0] = norm(vq[0, 0], qg[...]).astype(BF16)
    kv_out[0, 0] = norm(vk[0, 0], kg[...]).astype(BF16)
    kv_out[0, 1] = vv[0, 0]
    rows[pl.ds(i, 1), :] = norm(tq[...], qg[...])
    rows[pl.ds(HEADS + i, 1), :] = norm(tk[...], kg[...])
    rows[pl.ds(2 * HEADS + i, 1), :] = tv[...].astype(F32)

    @pl.when(i == HEADS - 1)
    def _():
        t_out[...] = rows[...].astype(BF16)


def post_kernel(order, vo, to, v_out, t_out):
    i = pl.program_id(0)
    v_out[0, 0] = vo[0]
    t_out[...] = to[pl.ds((i // 6) * 8 + i % 6, 1), :].astype(BF16)


def merge(o1, l1, o2, l2):
    top = jnp.maximum(l1, l2)
    w1 = jnp.exp2(l1 - top)
    w2 = jnp.exp2(l2 - top)
    total = w1 + w2
    return (o1 * w1 + o2 * w2) / total, top + jnp.log2(total)


def dot_t(a, b):
    return lax.dot_general(a, b, (((1,), (1,)), ((), ())), preferred_element_type=F32)


def attend(q, pieces):
    cc = math.log2(math.e) / math.sqrt(D)
    scores, peak = [], None
    for k, v, penalty, bias in pieces:
        s = dot_t(q, k)
        if bias is not None:
            s = s + bias
        scores.append(s)
        row = jnp.max(s, axis=-1, keepdims=True)
        if penalty is not None:
            row = row - penalty
        peak = row if peak is None else jnp.maximum(peak, row)
    peak = peak * cc
    total = None
    for s, (k, v, penalty, bias) in zip(scores, pieces):
        shift = peak if penalty is None else peak + penalty
        w = jnp.exp2(s * cc - shift).astype(BF16)
        ones = jnp.ones(v.shape, BF16)
        part = jnp.dot(w, jnp.concatenate([v, ones], axis=1), preferred_element_type=F32)
        total = part if total is None else total + part
    o, l = total[:, :D], total[:, D:]
    return o / l, peak + jnp.log2(l)


class Copy:
    def __init__(self, sems, number, src, dst, device, sends=None, receives=None):
        self.args = (src, dst, sems[0].at[number], sems[1].at[number])
        self.device, self.sends, self.receives = device, sends, receives

    def act(self, name, condition):
        def go():
            getattr(pltpu.make_async_remote_copy(
                *self.args, device_id=self.device, device_id_type=MESH), name)()
        if condition is None:
            go()
        else:
            pl.when(condition)(go)

    def start(self):
        self.act("start", self.sends)

    def wait_send(self):
        self.act("wait_send", self.sends)

    def wait_recv(self):
        self.act("wait_recv", self.receives)


def main_kernel(q_in, kv_in, t_in, tlen, v_out, t_out,
                q_all, kvg, o_own, l_own, o_send, l_send, o_got, l_got,
                tg, tf, tx, tp, ta, tb, td, te, rc, rx, ry, rz, re,
                own_sem, ssem, rsem, ret_s, ret_r):
    t = lax.axis_index("ta")
    s = lax.axis_index("sa")
    a, b, c = s // SW, s % SW, s % 2
    x, y, zh = s // 16, (s // 4) % 4, (s // 2) % 2
    z = zh * 4 + t
    has_out = jnp.where(c == 0, b > 0, b < SW - 1)
    mate = (t, s + 1 - 2 * c)
    outd = (t, s - 1 + 2 * c)
    t_up, t_dn, r_up, r_dn = t < 3, t > 0, a < 7, a > 0
    d_tup, d_tdn, d_rup, d_rdn = (t + 1, s), (t - 1, s), (t, s + SW), (t, s - SW)
    peers = {"x": [], "y": [], "z": []}
    for i in range(1, 4):
        x2, y2 = (x + i) % 4, (y + i) % 4
        peers["x"].append((x2, (t, s + 16 * (x2 - x))))
        peers["y"].append((y2, (t, s + 4 * (y2 - y))))
    for i in range(1, 8):
        z2 = (z + i) % 8
        peers["z"].append((z2, (z2 % 4, s + 2 * (z2 // 4 - zh))))

    bar = pltpu.get_barrier_semaphore()

    def greet(device, exists=None):
        def go():
            pl.semaphore_signal(bar, inc=1, device_id=device, device_id_type=MESH)
        if exists is None:
            go()
        else:
            pl.when(exists)(go)

    greet(mate)
    greet(outd, has_out)
    greet(d_tup, t_up)
    greet(d_tdn, t_dn)
    greet(d_rup, r_up)
    greet(d_rdn, r_dn)
    for axis in "xyz":
        for _, device in peers[axis]:
            greet(device)

    gi = c * 128 + (x * 4 + y) * 8 + z
    locals_ = [
        pltpu.make_async_copy(kv_in, kvg.at[pl.ds(0, HEADS), 0], own_sem.at[0]),
        pltpu.make_async_copy(q_in, q_all.at[0], own_sem.at[1]),
        pltpu.make_async_copy(t_in, tg.at[gi], own_sem.at[2]),
    ]
    for item in locals_:
        item.start()

    @pl.when(jnp.logical_not(has_out))
    def _():
        for h in range(8):
            kvg[h, 1] = jnp.zeros((2, TOK, D), BF16)
        for g in range(4):
            kvg[12 + g, 1] = jnp.zeros((2, TOK, D), BF16)

    @pl.when(jnp.logical_not(r_dn))
    def _():
        for h in range(8, 12):
            kvg[h, 1] = jnp.zeros((2, TOK, D), BF16)

    @pl.when(jnp.logical_not(r_up))
    def _():
        for h in range(8, 12):
            kvg[h, 2] = jnp.zeros((2, TOK, D), BF16)

    count = 14 + has_out.astype(jnp.int32) + t_up.astype(jnp.int32) + t_dn.astype(jnp.int32)
    count = count + r_up.astype(jnp.int32) + r_dn.astype(jnp.int32)
    pl.semaphore_wait(bar, count)

    sems = (ssem, rsem)
    number = [0]

    def copy(src, dst, device, sends=None, receives=None):
        number[0] += 1
        return Copy(sems, number[0] - 1, src, dst, device, sends, receives)

    def both(src, dst_low, dst_high, axis):
        if axis == "t":
            return [copy(src, dst_low, d_tup, t_up, t_dn), copy(src, dst_high, d_tdn, t_dn, t_up)]
        return [copy(src, dst_low, d_rup, r_up, r_dn), copy(src, dst_high, d_rdn, r_dn, r_up)]

    def heads(first, n):
        return pl.ds(first, n)

    out_c0 = copy(kv_in.at[heads(4, 2)], kvg.at[heads(4, 2), 1], outd, has_out, has_out)
    out_c12 = [copy(kv_in.at[heads(2, 2)], kvg.at[heads(2, 2), 1], outd, has_out, has_out),
               copy(kv_in.at[heads(6, 2)], kvg.at[heads(6, 2), 1], outd, has_out, has_out)]
    out_c4 = copy(kv_in.at[heads(0, 2)], kvg.at[heads(0, 2), 1], outd, has_out, has_out)
    mate_kv = copy(kv_in.at[heads(0, 8)], kvg.at[heads(0, 8), 2], mate)
    rows_kv = both(kv_in.at[heads(8, 4)], kvg.at[heads(8, 4), 1], kvg.at[heads(8, 4), 2], "r")
    relay_own = both(kv_in.at[4], kvg.at[12, 0], kvg.at[13, 0], "t") + both(kv_in.at[5], kvg.at[14, 0], kvg.at[15, 0], "r")

    def both_out(src, dst_low, dst_high, axis):
        up, dn, dev_up, dev_dn = (t_up, t_dn, d_tup, d_tdn) if axis == "t" else (r_up, r_dn, d_rup, d_rdn)
        return [copy(src, dst_low, dev_up, up & has_out, dn & has_out),
                copy(src, dst_high, dev_dn, dn & has_out, up & has_out)]

    relay_out = both_out(kvg.at[4, 1], kvg.at[12, 1], kvg.at[13, 1], "t") + both_out(kvg.at[5, 1], kvg.at[14, 1], kvg.at[15, 1], "r")
    exists = [t_dn, t_up, r_dn, r_up]
    relay_mate = [copy(kvg.at[12 + g, 0], kvg.at[12 + g, 2], mate, exists[g], exists[g]) for g in range(4)]
    q_row = both(q_in.at[heads(2, 3)], q_all.at[1, heads(2, 3)], q_all.at[2, heads(2, 3)], "r")
    q_time = both(q_in.at[heads(5, 5)], q_all.at[1, heads(5, 5)], q_all.at[2, heads(5, 5)], "t")
    g_z = [copy(tg.at[gi], tg.at[gi], device) for _, device in peers["z"]]
    base_y, base_x = c * 128 + (x * 4 + y) * 8, c * 128 + x * 32
    g_y = [copy(tg.at[pl.ds(base_y, 8)], tg.at[pl.ds(base_y, 8)], device) for _, device in peers["y"]]
    g_x = [copy(tg.at[pl.ds(base_x, 32)], tg.at[pl.ds(base_x, 32)], device) for _, device in peers["x"]]
    g_c = copy(tg.at[pl.ds(c * 128, 128)], tg.at[pl.ds(c * 128, 128)], mate)
    s_c = copy(tp.at[pl.ds(6 * (1 - c), 6)], rc, mate)
    s_x = [copy(ta.at[:, :, :, x2], rx.at[i], device) for i, (x2, device) in enumerate(peers["x"])]
    s_y = [copy(tb.at[:, :, :, pl.ds(8 * y2, 8)], ry.at[i], device) for i, (y2, device) in enumerate(peers["y"])]
    s_z = [copy(td.at[z2], rz.at[i], device) for i, (z2, device) in enumerate(peers["z"])]
    s_e = copy(te.at[pl.ds(8 * (1 - c), 8)], re, mate)

    def start(items):
        for item in items:
            item.start()

    def got(items):
        for item in items:
            item.wait_recv()

    def sent(items):
        for item in items:
            item.wait_send()

    for item in locals_:
        item.wait()
    start(g_z)
    start([out_c0])
    start(rows_kv + q_time + q_row + relay_own + [mate_kv] + out_c12 + [out_c4])

    pen_out = jnp.where(has_out, 0.0, BIG).astype(F32)
    pen_rdn = jnp.where(r_dn, 0.0, BIG).astype(F32)
    pen_rup = jnp.where(r_up, 0.0, BIG).astype(F32)
    bias_idx = lax.broadcasted_iota(jnp.int32, (1, TEXT), 1)
    i_c, i_x, i_y, i_z = bias_idx // 128, (bias_idx // 32) % 4, (bias_idx // 8) % 4, bias_idx % 8
    original = (i_z % 4) * 64 + i_x * 16 + i_y * 4 + (i_z // 4) * 2 + i_c
    text_bias = jnp.where(original < tlen[0], 0.0, -BIG).astype(F32)

    def text_arrived():
        def widen(i, _):
            tf[pl.ds(pl.multiple_of(i * 8 * TROWS, 8 * TROWS), 8 * TROWS)] = (
                tg[pl.ds(i * 8, 8)].astype(F32).reshape(8 * TROWS, D))
            return 0
        lax.fori_loop(0, TEXT // 8, widen, 0)

        def pick(j, _):
            tx[j] = tf[pl.ds(j, TEXT, stride=TROWS), :].astype(BF16)
            return 0
        lax.fori_loop(0, 3 * HEADS, pick, 0)

        def partial(h, _):
            o, l = attend(tx[h], [(kvg[h, 0, 0], kvg[h, 0, 1], None, None)])
            tp[h, 0] = o.reshape(2, 4, 32, D)
            tp[h, 1] = jnp.broadcast_to(l, (TEXT, D)).reshape(2, 4, 32, D)
            return 0
        lax.fori_loop(0, HEADS, partial, 0)

        @pl.when((t == 0) & (s == 0))
        def _():
            def self_part(h, _):
                o, l = attend(tx[h], [(tx[HEADS + h], tx[2 * HEADS + h], None, text_bias)])
                o, l = merge(tp[h, 0].reshape(TEXT, D), tp[h, 1].reshape(TEXT, D), o, l)
                tp[h, 0] = o.reshape(2, 4, 32, D)
                tp[h, 1] = l.reshape(2, 4, 32, D)
                return 0
            lax.fori_loop(0, HEADS, self_part, 0)

    def reduce_c():
        def one(h, _):
            o, l = merge(tp[6 * c + h, 0], tp[6 * c + h, 1], rc[h, 0], rc[h, 1])
            ta[h, 0] = o
            ta[h, 1] = l
            return 0
        lax.fori_loop(0, 6, one, 0)

    def reduce_x():
        def one(h, _):
            o, l = ta[h, 0, :, x], ta[h, 1, :, x]
            for i in range(3):
                o, l = merge(o, l, rx[i, h, 0], rx[i, h, 1])
            tb[h, 0] = o
            tb[h, 1] = l
            return 0
        lax.fori_loop(0, 6, one, 0)

    def reduce_y():
        for h in range(6):
            for cc in range(2):
                rows = pl.ds(pl.multiple_of(8 * y, 8), 8)
                o, l = tb[h, 0, cc, rows], tb[h, 1, cc, rows]
                for i in range(3):
                    o, l = merge(o, l, ry[i, h, 0, cc], ry[i, h, 1, cc])
                for k, value in enumerate((o, l)):
                    for zz in range(8):
                        td[zz, pl.ds(k * 16 + cc * 8 + h, 1), :] = value[zz:zz + 1]

    def reduce_z():
        o, l = td[z, pl.ds(0, 16)], td[z, pl.ds(16, 16)]
        for i in range(7):
            o, l = merge(o, l, rz[i, pl.ds(0, 16)], rz[i, pl.ds(16, 16)])
        te[...] = o

    def spread_out(l):
        return jnp.transpose(jnp.broadcast_to(l, (D, TOK)))

    def return_copies(h, d):
        row = h < 5
        dev_t = jnp.where(row, t, t - 1 + 2 * d)
        dev_s = jnp.where(row, s + (2 * d - 1) * SW, s)
        device = (dev_t, dev_s)
        return [
            pltpu.make_async_remote_copy(src_ref=o_send.at[d, h - 2], dst_ref=o_got.at[1 - d, h - 2],
                                         send_sem=ret_s.at[0, d, h - 2], recv_sem=ret_r.at[0, 1 - d, h - 2],
                                         device_id=device, device_id_type=MESH),
            pltpu.make_async_remote_copy(src_ref=l_send.at[d, h - 2], dst_ref=l_got.at[1 - d, h - 2],
                                         send_sem=ret_s.at[1, d, h - 2], recv_sem=ret_r.at[1, 1 - d, h - 2],
                                         device_id=device, device_id_type=MESH),
        ]

    def there(h, d):
        row = h < 5
        low = jnp.where(row, a, t) > 0
        high = jnp.where(row, a - 4, t) < 3
        return (h >= 2) & (h < 10) & jnp.where(d == 0, low, high)

    events = {
        0: lambda: (got(g_z), start(g_y), got(rows_kv), got(q_time)),
        1: lambda: (got(g_y), sent(g_z), start(g_x)),
        2: lambda: (got([out_c0]), start(relay_out)),
        3: lambda: (got(relay_own), start(relay_mate)),
        4: lambda: (got([mate_kv]), got(q_row), got(out_c12)),
        5: lambda: (got(g_x), sent(g_y), start([g_c])),
        6: lambda: (got([g_c]), text_arrived(), start([s_c])),
        7: lambda: (got([s_c]), reduce_c(), start(s_x)),
        8: lambda: (got(relay_out), got(relay_mate)),
        9: lambda: (got(s_x), reduce_x(), start(s_y)),
        10: lambda: (got([out_c4]),),
        11: lambda: (got(s_y), reduce_y(), start(s_z)),
    }

    def step(n, _):
        pair = n // 2
        first = jnp.where(pair == 0, 8, jnp.where(pair == 1, 10, jnp.where(pair == 2, 2, jnp.where(
            pair == 3, 6, jnp.where(pair == 4, 4, 0)))))
        h = first + n % 2
        for at, event in events.items():
            pl.when(n == at)(functools.partial(lambda event: event() and None, event))
        pen_a = jnp.where(h < 8, pen_out, pen_rdn)
        pen_b = jnp.where(h < 8, 0.0, pen_rup)
        relayed = pair == 4

        def one_query(qd, _):
            @pl.when((qd == 0) | there(h, qd - 1))
            def _():
                q = q_all[qd, h]

                def one_group(g, _):
                    group = jnp.where(g == 0, h, 12 + (h - 4) * 2 + g - 1)
                    present = jnp.where(h == 4, jnp.where(g == 1, t, 3 - t), jnp.where(g == 1, a, 7 - a)) > 0

                    @pl.when((g == 0) | present)
                    def _():
                        o, l = attend(q, [
                            (kvg[group, 0, 0], kvg[group, 0, 1], None, None),
                            (kvg[group, 1, 0], kvg[group, 1, 1], pen_a, None),
                            (kvg[group, 2, 0], kvg[group, 2, 1], pen_b, None),
                        ])

                        @pl.when(g == 0)
                        def _():
                            o_own[qd, h] = o
                            l_own[qd, h] = l

                        @pl.when(g > 0)
                        def _():
                            o2, l2 = merge(o_own[qd, h], l_own[qd, h], o, l)
                            o_own[qd, h] = o2
                            l_own[qd, h] = l2
                    return 0

                lax.fori_loop(0, jnp.where(relayed, 3, 1), one_group, 0)

                @pl.when(qd > 0)
                def _():
                    d = qd - 1
                    o_send[d, h - 2] = o_own[qd, h].astype(BF16)
                    l_send[d, h - 2] = jnp.transpose(l_own[qd, h])[:8]
                    for item in return_copies(h, d):
                        item.start()
            return 0

        lax.fori_loop(0, jnp.where((h >= 2) & (h < 10), 3, 1), one_query, 0)
        return 0

    lax.fori_loop(0, 12, step, 0)

    got(s_z)
    reduce_z()
    start([s_e])

    def finish(n, _):
        pair = n // 2
        first = jnp.where(pair == 0, 0, jnp.where(pair == 1, 10, jnp.where(pair == 2, 8, jnp.where(
            pair == 3, 2, jnp.where(pair == 4, 6, 4)))))
        h = first + n % 2
        o, l = attend(q_all[0, h], [(tx[HEADS + h], tx[2 * HEADS + h], None, text_bias)])
        o, l = merge(o_own[0, h], l_own[0, h], o, l)
        o_own[0, h] = o
        l_own[0, h] = l
        for d in range(2):
            @pl.when(there(h, d))
            def _():
                for item in return_copies(h, 1 - d):
                    item.wait_recv()
                o2, l2 = merge(o_own[0, h], l_own[0, h], o_got[d, h - 2].astype(F32),
                               spread_out(l_got[d, h - 2][:1]))
                o_own[0, h] = o2
                l_own[0, h] = l2
                for item in return_copies(h, d):
                    item.wait_send()
        v_out[h] = o_own[0, h].astype(BF16)
        return 0

    lax.fori_loop(0, 12, finish, 0)

    got([s_e])
    t_out[pl.ds(pl.multiple_of(8 * c, 8), 8), :] = te[pl.ds(pl.multiple_of(8 * c, 8), 8), :]
    t_out[pl.ds(pl.multiple_of(8 - 8 * c, 8), 8), :] = re[...]
    sent([out_c0, out_c4, mate_kv, g_c, s_c, s_e] + out_c12 + rows_kv + relay_own + relay_out + relay_mate)
    sent(q_row + q_time + g_x + s_x + s_y + s_z)


N_COPIES = 64


def main_call(q, kv, text, text_len):
    shapes = [
        pltpu.VMEM((3, HEADS, TOK, D), BF16),
        pltpu.VMEM((16, 3, 2, TOK, D), BF16),
        pltpu.VMEM((3, HEADS, TOK, D), F32),
        pltpu.VMEM((3, HEADS, TOK, D), F32),
        pltpu.VMEM((2, 8, TOK, D), BF16),
        pltpu.VMEM((2, 8, 8, TOK), F32),
        pltpu.VMEM((2, 8, TOK, D), BF16),
        pltpu.VMEM((2, 8, 8, TOK), F32),
        pltpu.VMEM((TEXT, TROWS, D), BF16),
        pltpu.VMEM((TEXT * TROWS, D), F32),
        pltpu.VMEM((3 * HEADS, TEXT, D), BF16),
        pltpu.VMEM((HEADS, 2, 2, 4, 32, D), F32),
        pltpu.VMEM((6, 2, 2, 4, 32, D), F32),
        pltpu.VMEM((6, 2, 2, 32, D), F32),
        pltpu.VMEM((8, 32, D), F32),
        pltpu.VMEM((16, D), F32),
        pltpu.VMEM((6, 2, 2, 4, 32, D), F32),
        pltpu.VMEM((3, 6, 2, 2, 32, D), F32),
        pltpu.VMEM((3, 6, 2, 2, 8, D), F32),
        pltpu.VMEM((7, 32, D), F32),
        pltpu.VMEM((8, D), F32),
        pltpu.SemaphoreType.DMA((3,)),
        pltpu.SemaphoreType.DMA((N_COPIES,)),
        pltpu.SemaphoreType.DMA((N_COPIES,)),
        pltpu.SemaphoreType.DMA((2, 2, 8)),
        pltpu.SemaphoreType.DMA((2, 2, 8)),
    ]
    anywhere = pl.BlockSpec(memory_space=pl.ANY)
    return pl.pallas_call(
        main_kernel,
        out_shape=(jax.ShapeDtypeStruct((HEADS, TOK, D), BF16), jax.ShapeDtypeStruct((16, D), F32)),
        in_specs=[anywhere, anywhere, anywhere, pl.BlockSpec(memory_space=pltpu.SMEM)],
        out_specs=(pl.BlockSpec(memory_space=pltpu.VMEM), pl.BlockSpec(memory_space=pltpu.VMEM)),
        scratch_shapes=shapes,
        compiler_params=pltpu.CompilerParams(
            collective_id=0, has_side_effects=True, vmem_limit_bytes=VMEM_LIMIT),
        name="tiles",
    )(q, kv, text, text_len)


def local(video_q, video_k, video_v, text_q, text_k, text_v, q_gain, k_gain, text_len, window):
    wide = (window == 3).astype(jnp.int32)
    code = wide[:, 0] * 4 + wide[:, 1] * 2 + wide[:, 2]
    rank = jnp.zeros_like(code)
    for value, place in enumerate(RANK_OF_CODE):
        rank = jnp.where(code == value, place, rank)
    key = rank * HEADS + jnp.arange(HEADS, dtype=jnp.int32)
    position = jnp.sum((key[None, :] < key[:, None]).astype(jnp.int32), axis=1)
    places = jnp.arange(HEADS, dtype=jnp.int32)
    order = jnp.sum(jnp.where(position[None, :] == places[:, None], places[None, :], 0), axis=1)

    tile = pl.BlockSpec((1, 1, TOK, D), lambda i, order: (0, 0, 0, order[i]))
    row = pl.BlockSpec((1, D), lambda i, order: (0, order[i]))
    gain = pl.BlockSpec((1, D), lambda i, order: (0, 0))
    q, kv, text = pl.pallas_call(
        pre_kernel,
        grid_spec=pltpu.PrefetchScalarGridSpec(
            num_scalar_prefetch=1, grid=(HEADS,),
            in_specs=[tile, tile, tile, row, row, row, gain, gain],
            out_specs=[
                pl.BlockSpec((1, TOK, D), lambda i, order: (i, 0, 0)),
                pl.BlockSpec((1, 2, TOK, D), lambda i, order: (i, 0, 0, 0)),
                pl.BlockSpec((TROWS, D), lambda i, order: (0, 0)),
            ],
            scratch_shapes=[pltpu.VMEM((TROWS, D), F32)],
        ),
        out_shape=(jax.ShapeDtypeStruct((HEADS, TOK, D), BF16), jax.ShapeDtypeStruct((HEADS, 2, TOK, D), BF16),
                   jax.ShapeDtypeStruct((TROWS, D), BF16)),
        name="prepare",
    )(order, video_q, video_k, video_v, text_q, text_k, text_v, q_gain[None], k_gain[None])

    video, text_rows = main_call(q, kv, text, text_len)

    return tuple(pl.pallas_call(
        post_kernel,
        grid_spec=pltpu.PrefetchScalarGridSpec(
            num_scalar_prefetch=1, grid=(HEADS,),
            in_specs=[pl.BlockSpec((1, TOK, D), lambda i, order: (i, 0, 0)),
                      pl.BlockSpec((16, D), lambda i, order: (0, 0))],
            out_specs=[tile, row],
        ),
        out_shape=(jax.ShapeDtypeStruct(video_q.shape, BF16), jax.ShapeDtypeStruct(text_q.shape, BF16)),
        name="place",
    )(order, video, text_rows))


def solution(mesh):
    tiles, rows = P("ta", "sa", None, None), P(("ta", "sa"), None)
    return jax.shard_map(
        local, mesh=mesh,
        in_specs=(tiles, tiles, tiles, rows, rows, rows, P(), P(), P(), P()),
        out_specs=(tiles, rows),
        check_vma=False,
    )
```

```python
import functools
import math

import jax
import jax.numpy as jnp
from jax import lax
from jax.experimental import pallas as pl
from jax.experimental.pallas import tpu as pltpu
from jax.sharding import PartitionSpec as P

MESH = pl.DeviceIdType.MESH
EPS = 1e-6
F32, BF16 = jnp.float32, jnp.bfloat16
HEADS, D, TOK, TEXT = 12, 128, 384, 256
SW = 8
BIG = 1e30
TROWS = 48
VMEM_LIMIT = 61 * 2**20
RANK_OF_CODE = (0, 0, 5, 1, 0, 3, 4, 2)


def merge(o1, l1, o2, l2):
    top = jnp.maximum(l1, l2)
    w1 = jnp.exp2(l1 - top)
    w2 = jnp.exp2(l2 - top)
    total = w1 + w2
    return (o1 * w1 + o2 * w2) / total, top + jnp.log2(total)


def dot_t(a, b):
    return lax.dot_general(a, b, (((1,), (1,)), ((), ())), preferred_element_type=F32)


def attend(q, pieces):
    cc = math.log2(math.e) / math.sqrt(D)
    scores, peak = [], None
    for k, v, penalty, bias in pieces:
        s = dot_t(q, k)
        if bias is not None:
            s = s + bias
        scores.append(s)
        row = jnp.max(s, axis=-1, keepdims=True)
        if penalty is not None:
            row = row - penalty
        peak = row if peak is None else jnp.maximum(peak, row)
    peak = peak * cc
    total = None
    for s, (k, v, penalty, bias) in zip(scores, pieces):
        shift = peak if penalty is None else peak + penalty
        w = jnp.exp2(s * cc - shift).astype(BF16)
        ones = jnp.ones(v.shape, BF16)
        part = jnp.dot(w, jnp.concatenate([v, ones], axis=1), preferred_element_type=F32)
        total = part if total is None else total + part
    o, l = total[:, :D], total[:, D:]
    return o / l, peak + jnp.log2(l)


class Copy:
    def __init__(self, sems, number, src, dst, device, sends=None, receives=None):
        self.args = (src, dst, sems[0].at[number], sems[1].at[number])
        self.device, self.sends, self.receives = device, sends, receives

    def act(self, name, condition):
        def go():
            getattr(pltpu.make_async_remote_copy(
                *self.args, device_id=self.device, device_id_type=MESH), name)()
        if condition is None:
            go()
        else:
            pl.when(condition)(go)

    def start(self):
        self.act("start", self.sends)

    def wait_send(self):
        self.act("wait_send", self.sends)

    def wait_recv(self):
        self.act("wait_recv", self.receives)


def main_kernel(order, place, tlen, vq, vk, vv, tq, tk, tv, qg, kg, v_out, t_out,
                q_all, kvg, rbuf, o_own, l_own, o_send, l_send, o_got, l_got, final,
                raw, raw_t, rows, tg, tf, tx, tpo, tpl, tao, tal, tb, td, te, rco, rcl, rxo, rxl, ry, rz, tr, ends,
                ssem, rsem, ret_s, ret_r):
    t = lax.axis_index("ta")
    s = lax.axis_index("sa")
    a, b, c = s // SW, s % SW, s % 2
    x, y, zh = s // 16, (s // 4) % 4, (s // 2) % 2
    z = zh * 4 + t
    even = a % 2 == 0
    has_out = jnp.where(c == 0, b > 0, b < SW - 1)
    middle, edge = (b == 3) | (b == 4), (b == 0) | (b == SW - 1)
    has_far = jnp.where(even, a >= 2, a <= 5)
    far_send = jnp.where(even, a <= 4, a >= 3)
    t_up, t_dn, r_up, r_dn = t < 3, t > 0, a < 7, a > 0
    mate = (t, s + 1 - 2 * c)
    outd = (t, s - 1 + 2 * c)
    d_tup, d_tdn, d_rup, d_rdn = (t + 1, s), (t - 1, s), (t, s + SW), (t, s - SW)
    pair = (t, jnp.where(even, s + SW, s - SW))
    fard = (t, jnp.where(even, s + 2 * SW, s - 2 * SW))
    via = (t, jnp.where(b == 3, s + 4, s - 4))
    hop = (t, jnp.where(b % 4 == 0, s + 3, s - 3))
    peers = {"x": [], "y": [], "z": []}
    for i in range(1, 4):
        x2, y2 = (x + i) % 4, (y + i) % 4
        peers["x"].append((x2, (t, s + 16 * (x2 - x))))
        peers["y"].append((y2, (t, s + 4 * (y2 - y))))
    for i in range(1, 8):
        z2 = (z + i) % 8
        peers["z"].append((z2, (z2 % 4, s + 2 * (z2 // 4 - zh))))

    bar = pltpu.get_barrier_semaphore()

    def greet(device, exists=None):
        def go():
            pl.semaphore_signal(bar, inc=1, device_id=device, device_id_type=MESH)
        if exists is None:
            go()
        else:
            pl.when(exists)(go)

    greet(mate)
    greet(outd, has_out)
    greet(hop, middle | edge)
    greet(d_tup, t_up)
    greet(d_tdn, t_dn)
    greet(d_rup, r_up)
    greet(d_rdn, r_dn)
    for axis in "xyz":
        for _, device in peers[axis]:
            greet(device)

    sems = (ssem, rsem)
    number = [0]

    def copy(src, dst, device, sends=None, receives=None):
        number[0] += 1
        return Copy(sems, number[0] - 1, src, dst, device, sends, receives)

    def both(src, dst_low, dst_high, axis):
        if axis == "t":
            return [copy(src, dst_low, d_tup, t_up, t_dn), copy(src, dst_high, d_tdn, t_dn, t_up)]
        return [copy(src, dst_low, d_rup, r_up, r_dn), copy(src, dst_high, d_rdn, r_dn, r_up)]

    def slot(first, n, piece):
        return kvg.at[pl.ds(first, n), piece]

    out_c0 = copy(slot(4, 2, 0), slot(4, 2, 1), outd, has_out, has_out)
    out_c2 = copy(slot(6, 2, 0), slot(6, 2, 1), outd, has_out, has_out)
    near = has_out & jnp.logical_not(middle)
    out_c1, via_c1, hop_c1 = (copy(slot(2, 2, 0), slot(2, 2, 1), outd, near, near),
                              copy(slot(2, 2, 0), rbuf.at[pl.ds(2, 2)], via, middle, edge),
                              copy(rbuf.at[pl.ds(2, 2)], slot(2, 2, 1), hop, edge, middle))
    out_c4, via_c4, hop_c4 = (copy(slot(0, 2, 0), slot(0, 2, 1), outd, near, near),
                              copy(slot(0, 2, 0), rbuf.at[pl.ds(0, 2)], via, middle, edge),
                              copy(rbuf.at[pl.ds(0, 2)], slot(0, 2, 1), hop, edge, middle))
    mate_kv = copy(slot(0, 8, 0), slot(0, 8, 2), mate)
    rows_pair = copy(slot(8, 4, 0), slot(8, 4, 1), pair)
    rows_far = copy(slot(8, 4, 1), slot(8, 4, 2), fard, far_send, has_far)
    own_pair = copy(slot(4, 2, 0), slot(12, 2, 0), pair)
    own_far = copy(slot(12, 2, 0), slot(14, 2, 0), fard, far_send, has_far)
    out_pair = copy(slot(4, 2, 1), slot(12, 2, 1), pair, has_out, has_out)
    out_far = copy(slot(12, 2, 1), slot(14, 2, 1), fard, far_send & has_out, has_far & has_out)
    mate_pair = copy(slot(12, 2, 0), slot(12, 2, 2), mate)
    mate_far = copy(slot(14, 2, 0), slot(14, 2, 2), mate, has_far, has_far)
    q_row = both(q_all.at[0, pl.ds(2, 2)], q_all.at[1, pl.ds(2, 2)], q_all.at[2, pl.ds(2, 2)], "r")
    q_time = both(q_all.at[0, pl.ds(4, 6)], q_all.at[1, pl.ds(4, 6)], q_all.at[2, pl.ds(4, 6)], "t")
    gi = y * 8 + z
    g_z = [copy(tg.at[gi], tg.at[gi], device) for _, device in peers["z"]]
    g_y = [copy(tg.at[pl.ds(y * 8, 8)], tg.at[pl.ds(y * 8, 8)], device) for _, device in peers["y"]]
    g_x = [copy(tx.at[:, c, x], tx.at[:, c, x], device) for _, device in peers["x"]]
    g_c = copy(tx.at[:, c], tx.at[:, c], mate)
    s_c = [copy(tpo.at[pl.ds(6 * (1 - c), 6)], rco, mate), copy(tpl.at[1 - c], rcl, mate)]
    s_x = [copy(tao.at[:, :, x2], rxo.at[i], device) for i, (x2, device) in enumerate(peers["x"])]
    s_x += [copy(tal.at[:, x2], rxl.at[i], device) for i, (x2, device) in enumerate(peers["x"])]
    s_y = [copy(tb.at[:, :, :, pl.ds(8 * y2, 8)], ry.at[i], device) for i, (y2, device) in enumerate(peers["y"])]
    s_z = [copy(td.at[z2], rz.at[i], device) for i, (z2, device) in enumerate(peers["z"])]
    s_e = copy(te.at[pl.ds(8 * (1 - c), 8)], tr, mate)

    def start(*items):
        for item in items:
            item.start()

    def got(*items):
        for item in items:
            item.wait_recv()

    def norm(value, gain):
        u = value.astype(F32)
        return u * lax.rsqrt(jnp.mean(u * u, axis=-1, keepdims=True) + EPS) * gain[...]

    for h in range(HEADS):
        here = pl.ds(h * D, D)
        raw_t[h] = jnp.broadcast_to(norm(tq[:, here], qg), (8, D))
        raw_t[HEADS + h] = jnp.broadcast_to(norm(tk[:, here], kg), (8, D))
        raw_t[2 * HEADS + h] = jnp.broadcast_to(tv[:, here].astype(F32), (8, D))
    for k, ref in enumerate((vk, vv, vq)):
        for h in range(HEADS):
            raw[k, h] = ref[0, 0, :, pl.ds(h * D, D)]

    def prepare_q(first, n):
        def one(p, _):
            q_all[0, p] = norm(raw[2, order[p]], qg).astype(BF16)
            return 0
        lax.fori_loop(first, first + n, one, 0)

    def prepare_kv(first, n):
        def one(p, _):
            kvg[p, 0, 0] = norm(raw[0, order[p]], kg).astype(BF16)
            kvg[p, 0, 1] = raw[1, order[p]]
            return 0
        lax.fori_loop(first, first + n, one, 0)

    def prepare_text(p, _):
        h = order[p]
        for k in range(3):
            rows[pl.ds(k * HEADS + p, 1), :] = raw_t[k * HEADS + h][:1]
        return 0

    rows[...] = jnp.zeros_like(rows)
    lax.fori_loop(0, HEADS, prepare_text, 0)
    tg[gi] = rows[...].astype(BF16)
    prepare_kv(4, 2)

    count = 14 + has_out.astype(jnp.int32) + t_up.astype(jnp.int32) + t_dn.astype(jnp.int32)
    count = count + r_up.astype(jnp.int32) + r_dn.astype(jnp.int32) + (middle | edge).astype(jnp.int32)
    pl.semaphore_wait(bar, count)

    start(*g_z, out_c0, own_pair)
    prepare_q(4, 6)
    start(*q_time)
    prepare_kv(8, 4)
    start(rows_pair)
    prepare_kv(2, 2)
    start(out_c1, via_c1)
    prepare_kv(6, 2)
    start(out_c2)
    prepare_q(2, 2)
    start(*q_row)
    prepare_kv(0, 2)
    start(out_c4, via_c4, mate_kv)
    prepare_q(0, 2)
    prepare_q(10, 2)

    @pl.when(jnp.logical_not(has_out))
    def _():
        def clear(i, _):
            kvg[jnp.where(i < 8, i, i + 4), 1] = jnp.zeros((2, TOK, D), BF16)
            return 0
        lax.fori_loop(0, 12, clear, 0)

    @pl.when(jnp.logical_not(has_far))
    def _():
        def clear(i, _):
            kvg[8 + i, 2] = jnp.zeros((2, TOK, D), BF16)
            return 0
        lax.fori_loop(0, 4, clear, 0)

    got(*g_z)
    start(*g_y)
    got(rows_pair)
    start(rows_far)

    pen_out = jnp.where(has_out, 0.0, BIG).astype(F32)
    pen_far = jnp.where(has_far, 0.0, BIG).astype(F32)
    index = lax.broadcasted_iota(jnp.int32, (1, TEXT), 1)
    i_c, i_x, i_y, i_z = index // 128, (index // 32) % 4, (index // 8) % 4, index % 8
    original = (i_z % 4) * 64 + i_x * 16 + i_y * 4 + (i_z // 4) * 2 + i_c
    text_bias = jnp.where(original < tlen[0], 0.0, -BIG).astype(F32)
    lane = lax.broadcasted_iota(jnp.int32, (1, D), 1) // 16

    def packed(l, h, old):
        return jnp.where(lane == h, l, old)

    def unpacked(l, h):
        return jnp.sum(jnp.where((lane == h) & (lax.broadcasted_iota(jnp.int32, (1, D), 1) % 16 == 0), l, 0.0),
                       axis=-1, keepdims=True)

    def text(j):
        return tx[j].reshape(TEXT, D)

    def sort_text():
        def widen(i, _):
            tf[pl.ds(pl.multiple_of(i * 8 * TROWS, 8 * TROWS), 8 * TROWS)] = (
                tg[pl.ds(i * 8, 8)].astype(F32).reshape(8 * TROWS, D))
            return 0
        lax.fori_loop(0, 4, widen, 0)

        def pick(j, _):
            tx[j, c, x] = tf[pl.ds(j, 32, stride=TROWS), :].astype(BF16)
            return 0
        lax.fori_loop(0, 3 * HEADS, pick, 0)

    def text_partial():
        for half in range(2):
            def partial(i, l_packed):
                h = half * 6 + i
                o, l = attend(text(h), [(kvg[h, 0, 0], kvg[h, 0, 1], None, None)])
                tpo[h] = o.astype(BF16).reshape(2, 4, 32, D)
                return packed(l, i, l_packed)
            tpl[half] = lax.fori_loop(0, 6, partial, jnp.zeros((TEXT, D), F32)).reshape(2, 4, 32, D)

        @pl.when((t == 0) & (s == 0))
        def _():
            for half in range(2):
                def self_part(i, _):
                    h = half * 6 + i
                    o, l = attend(text(h), [(text(HEADS + h), text(2 * HEADS + h), None, text_bias)])
                    l_packed = tpl[half].reshape(TEXT, D)
                    o, l = merge(tpo[h].reshape(TEXT, D).astype(F32), unpacked(l_packed, i), o, l)
                    tpo[h] = o.astype(BF16).reshape(2, 4, 32, D)
                    tpl[half] = packed(l, i, l_packed).reshape(2, 4, 32, D)
                    return 0
                lax.fori_loop(0, 6, self_part, 0)

    def reduce_c():
        def one(h, l_packed):
            o, l = merge(tpo[6 * c + h].reshape(TEXT, D).astype(F32), unpacked(tpl[c].reshape(TEXT, D), h),
                         rco[h].reshape(TEXT, D).astype(F32), unpacked(rcl[...].reshape(TEXT, D), h))
            tao[h] = o.astype(BF16).reshape(2, 4, 32, D)
            return packed(l, h, l_packed)
        tal[...] = lax.fori_loop(0, 6, one, jnp.zeros((TEXT, D), F32)).reshape(2, 4, 32, D)

    def reduce_x():
        def one(h, _):
            o, l = tao[h, :, x].reshape(64, D).astype(F32), unpacked(tal[:, x].reshape(64, D), h)
            for i in range(3):
                o, l = merge(o, l, rxo[i, h].reshape(64, D).astype(F32), unpacked(rxl[i].reshape(64, D), h))
            tb[h, 0] = o.reshape(2, 32, D)
            tb[h, 1] = jnp.broadcast_to(l, (64, D)).reshape(2, 32, D)
            return 0
        lax.fori_loop(0, 6, one, 0)

    def reduce_y():
        for h in range(6):
            for cc in range(2):
                eight = pl.ds(pl.multiple_of(8 * y, 8), 8)
                o, l = tb[h, 0, cc, eight], tb[h, 1, cc, eight]
                for i in range(3):
                    o, l = merge(o, l, ry[i, h, 0, cc], ry[i, h, 1, cc])
                for k, value in enumerate((o, l)):
                    for zz in range(8):
                        td[zz, pl.ds(k * 16 + cc * 8 + h, 1), :] = value[zz:zz + 1]

    def reduce_z():
        o, l = td[z, pl.ds(0, 16)], td[z, pl.ds(16, 16)]
        for i in range(7):
            o, l = merge(o, l, rz[i, pl.ds(0, 16)], rz[i, pl.ds(16, 16)])
        te[...] = o

    def spread_out(l):
        return jnp.transpose(jnp.broadcast_to(l, (D, TOK)))

    def return_copies(h, d):
        row = h < 4
        dev_t = jnp.where(row, t, t - 1 + 2 * d)
        dev_s = jnp.where(row, s + (2 * d - 1) * SW, s)
        device = (dev_t, dev_s)
        return [
            pltpu.make_async_remote_copy(src_ref=o_send.at[d, h - 2], dst_ref=o_got.at[1 - d, h - 2],
                                         send_sem=ret_s.at[0, d, h - 2], recv_sem=ret_r.at[0, 1 - d, h - 2],
                                         device_id=device, device_id_type=MESH),
            pltpu.make_async_remote_copy(src_ref=l_send.at[d, h - 2], dst_ref=l_got.at[1 - d, h - 2],
                                         send_sem=ret_s.at[1, d, h - 2], recv_sem=ret_r.at[1, 1 - d, h - 2],
                                         device_id=device, device_id_type=MESH),
        ]

    def there(h, d):
        row = h < 4
        low = jnp.where(row, a, t) > 0
        high = jnp.where(row, a - 4, t) < 3
        return (h >= 2) & (h < 10) & jnp.where(d == 0, low, high)

    events = {
        0: lambda: (got(*g_y), sort_text(), start(*g_x), got(rows_far, *q_time)),
        1: lambda: (got(own_pair), start(own_far, mate_pair), got(via_c1), start(hop_c1)),
        2: lambda: (got(out_c0), start(out_pair)),
        3: lambda: (got(*g_x), start(g_c), got(own_far), start(mate_far), got(via_c4), start(hop_c4)),
        4: lambda: (got(g_c), text_partial(), start(*s_c), got(mate_kv, out_c1, hop_c1, *q_row)),
        5: lambda: (got(out_pair), start(out_far), got(*s_c), reduce_c(), start(*s_x)),
        6: lambda: (got(out_c2),),
        8: lambda: (got(*s_x), reduce_x(), start(*s_y), got(out_far, mate_pair, mate_far)),
        9: lambda: (got(*s_y), reduce_y(), start(*s_z)),
        10: lambda: (got(*s_z), reduce_z(), start(s_e), got(out_c4, hop_c4)),
    }

    def step(n, _):
        duo = n // 2
        first = jnp.where(duo == 0, 8, jnp.where(duo == 1, 10, jnp.where(duo == 2, 2, jnp.where(
            duo == 3, 6, jnp.where(duo == 4, 4, 0)))))
        h = first + n % 2
        for at, event in events.items():
            pl.when(n == at)(functools.partial(lambda event: event() and None, event))
        pen_a = jnp.where(h < 8, pen_out, 0.0)
        pen_b = jnp.where(h < 8, 0.0, pen_far)
        relayed = duo == 4

        def one_query(qd, _):
            @pl.when((qd == 0) | there(h, qd - 1))
            def _():
                q = q_all[qd, h]

                def one_group(g, _):
                    group = h + jnp.where(g == 0, 0, 6 + 2 * g)

                    @pl.when((g < 2) | has_far)
                    def _():
                        o, l = attend(q, [
                            (kvg[group, 0, 0], kvg[group, 0, 1], None, None),
                            (kvg[group, 1, 0], kvg[group, 1, 1], pen_a, None),
                            (kvg[group, 2, 0], kvg[group, 2, 1], pen_b, None),
                        ])

                        @pl.when(g == 0)
                        def _():
                            o_own[qd, h] = o
                            l_own[qd, h] = l

                        @pl.when(g > 0)
                        def _():
                            o2, l2 = merge(o_own[qd, h], l_own[qd, h], o, l)
                            o_own[qd, h] = o2
                            l_own[qd, h] = l2
                    return 0

                lax.fori_loop(0, jnp.where(relayed, 3, 1), one_group, 0)

                @pl.when(qd > 0)
                def _():
                    d = qd - 1
                    o_send[d, h - 2] = o_own[qd, h].astype(BF16)
                    l_send[d, h - 2] = jnp.transpose(l_own[qd, h])[:8]
                    for item in return_copies(h, d):
                        item.start()
            return 0

        lax.fori_loop(0, jnp.where((h >= 2) & (h < 10), 3, 1), one_query, 0)
        return 0

    lax.fori_loop(0, 12, step, 0)

    def finish(n, _):
        duo = n // 2
        first = jnp.where(duo == 0, 0, jnp.where(duo == 1, 10, jnp.where(duo == 2, 8, jnp.where(
            duo == 3, 2, jnp.where(duo == 4, 6, 4)))))
        h = first + n % 2
        o, l = attend(q_all[0, h], [(text(HEADS + h), text(2 * HEADS + h), None, text_bias)])
        o, l = merge(o_own[0, h], l_own[0, h], o, l)
        o_own[0, h] = o
        l_own[0, h] = l
        for d in range(2):
            @pl.when(there(h, d))
            def _():
                for item in return_copies(h, 1 - d):
                    item.wait_recv()
                o2, l2 = merge(o_own[0, h], l_own[0, h], o_got[d, h - 2].astype(F32),
                               spread_out(l_got[d, h - 2][:1]))
                o_own[0, h] = o2
                l_own[0, h] = l2
                for item in return_copies(h, d):
                    item.wait_send()
        final[h] = o_own[0, h].astype(BF16)
        return 0

    lax.fori_loop(0, 12, finish, 0)

    got(s_e)
    mine = te[pl.ds(pl.multiple_of(8 * c, 8), 8), :]
    for i in range(6):
        ends[6 * c + i] = jnp.broadcast_to(mine[i:i + 1], (8, D))
        ends[6 * (1 - c) + i] = jnp.broadcast_to(tr[i:i + 1, :], (8, D))
    for h in range(HEADS):
        p = place[h]
        here = pl.ds(h * D, D)
        v_out[0, 0, :, here] = final[p]
        t_out[:, here] = ends[p][:1].astype(BF16)
    for item in ([out_c0, out_c1, out_c2, out_c4, via_c1, via_c4, hop_c1, hop_c4, mate_kv, rows_pair, rows_far, own_pair,
                  own_far, out_pair, out_far, mate_pair, mate_far, g_c, s_e]
                 + q_row + q_time + g_z + g_y + g_x + s_c + s_x + s_y + s_z):
        item.wait_send()


N_COPIES = 64


def main_call(order, place, text_len, arrays):
    shapes = [
        pltpu.VMEM((3, HEADS, TOK, D), BF16),
        pltpu.VMEM((16, 3, 2, TOK, D), BF16),
        pltpu.VMEM((4, 2, TOK, D), BF16),
        pltpu.VMEM((3, HEADS, TOK, D), F32),
        pltpu.VMEM((3, HEADS, TOK, D), F32),
        pltpu.VMEM((2, 8, TOK, D), BF16),
        pltpu.VMEM((2, 8, 8, TOK), F32),
        pltpu.VMEM((2, 8, TOK, D), BF16),
        pltpu.VMEM((2, 8, 8, TOK), F32),
        pltpu.VMEM((HEADS, TOK, D), BF16),
        pltpu.VMEM((3, HEADS, TOK, D), BF16),
        pltpu.VMEM((3 * HEADS, 8, D), F32),
        pltpu.VMEM((TROWS, D), F32),
        pltpu.VMEM((32, TROWS, D), BF16),
        pltpu.VMEM((32 * TROWS, D), F32),
        pltpu.VMEM((3 * HEADS, 2, 4, 32, D), BF16),
        pltpu.VMEM((HEADS, 2, 4, 32, D), BF16),
        pltpu.VMEM((2, 2, 4, 32, D), F32),
        pltpu.VMEM((6, 2, 4, 32, D), BF16),
        pltpu.VMEM((2, 4, 32, D), F32),
        pltpu.VMEM((6, 2, 2, 32, D), F32),
        pltpu.VMEM((8, 32, D), F32),
        pltpu.VMEM((16, D), F32),
        pltpu.VMEM((6, 2, 4, 32, D), BF16),
        pltpu.VMEM((2, 4, 32, D), F32),
        pltpu.VMEM((3, 6, 2, 32, D), BF16),
        pltpu.VMEM((3, 2, 32, D), F32),
        pltpu.VMEM((3, 6, 2, 2, 8, D), F32),
        pltpu.VMEM((7, 32, D), F32),
        pltpu.VMEM((8, D), F32),
        pltpu.VMEM((HEADS, 8, D), F32),
        pltpu.SemaphoreType.DMA((N_COPIES,)),
        pltpu.SemaphoreType.DMA((N_COPIES,)),
        pltpu.SemaphoreType.DMA((2, 2, 8)),
        pltpu.SemaphoreType.DMA((2, 2, 8)),
    ]
    scalars, vmem = pl.BlockSpec(memory_space=pltpu.SMEM), pl.BlockSpec(memory_space=pltpu.VMEM)
    return pl.pallas_call(
        main_kernel,
        out_shape=(jax.ShapeDtypeStruct(arrays[0].shape, BF16), jax.ShapeDtypeStruct(arrays[3].shape, BF16)),
        in_specs=[scalars] * 3 + [vmem] * 8,
        out_specs=(vmem, vmem),
        scratch_shapes=shapes,
        compiler_params=pltpu.CompilerParams(
            collective_id=0, has_side_effects=True, vmem_limit_bytes=VMEM_LIMIT),
        name="tiles",
    )(order, place, text_len, *arrays)


def local(video_q, video_k, video_v, text_q, text_k, text_v, q_gain, k_gain, text_len, window):
    wide = (window == 3).astype(jnp.int32)
    code = wide[:, 0] * 4 + wide[:, 1] * 2 + wide[:, 2]
    rank = jnp.zeros_like(code)
    for value, place in enumerate(RANK_OF_CODE):
        rank = jnp.where(code == value, place, rank)
    key = rank * HEADS + jnp.arange(HEADS, dtype=jnp.int32)
    position = jnp.sum((key[None, :] < key[:, None]).astype(jnp.int32), axis=1)
    places = jnp.arange(HEADS, dtype=jnp.int32)
    order = jnp.sum(jnp.where(position[None, :] == places[:, None], places[None, :], 0), axis=1)

    return main_call(order, position, text_len, (
        video_q, video_k, video_v, text_q, text_k, text_v, q_gain[None], k_gain[None]))


def solution(mesh):
    tiles, rows = P("ta", "sa", None, None), P(("ta", "sa"), None)
    return jax.shard_map(
        local, mesh=mesh,
        in_specs=(tiles, tiles, tiles, rows, rows, rows, P(), P(), P(), P()),
        out_specs=(tiles, rows),
        check_vma=False,
    )
```

```python
import functools
import math

import jax
import jax.numpy as jnp
from jax import lax
from jax.experimental import pallas as pl
from jax.experimental.pallas import tpu as pltpu
from jax.sharding import PartitionSpec as P

MESH = pl.DeviceIdType.MESH
EPS = 1e-6
F32, BF16 = jnp.float32, jnp.bfloat16
HEADS, D, TOK, TEXT = 12, 128, 384, 256
SW = 8
BIG = 1e30
TROWS = 48
VMEM_LIMIT = 61 * 2**20
RANK_OF_CODE = (0, 0, 5, 1, 0, 3, 4, 2)


def merge(o1, l1, o2, l2):
    top = jnp.maximum(l1, l2)
    w1 = jnp.exp2(l1 - top)
    w2 = jnp.exp2(l2 - top)
    total = w1 + w2
    return (o1 * w1 + o2 * w2) / total, top + jnp.log2(total)


def dot_t(a, b):
    return lax.dot_general(a, b, (((1,), (1,)), ((), ())), preferred_element_type=F32)


def attend(q, pieces, bias=None):
    cc = math.log2(math.e) / math.sqrt(D)
    scores, peak = [], None
    for k, v in pieces:
        s = dot_t(q, k)
        if bias is not None:
            s = s + bias
        scores.append(s)
        row = jnp.max(s, axis=-1, keepdims=True)
        peak = row if peak is None else jnp.maximum(peak, row)
    peak = peak * cc
    total = None
    for s, (k, v) in zip(scores, pieces):
        w = jnp.exp2(s * cc - peak).astype(BF16)
        part = jnp.dot(w, jnp.concatenate([v, jnp.ones(v.shape, BF16)], axis=1), preferred_element_type=F32)
        total = part if total is None else total + part
    o, l = total[:, :D], total[:, D:]
    return o / l, peak + jnp.log2(l)


def absorb(q, pieces, state, bias=None):
    cc = math.log2(math.e) / math.sqrt(D)
    acc, l, m = state
    scores, peak = [], None
    for k, v in pieces:
        s = dot_t(q, k)
        if bias is not None:
            s = s + bias
        scores.append(s)
        for i in range(0, s.shape[1], D):
            part = s[:, i:i + D]
            peak = part if peak is None else jnp.maximum(peak, part)
    new = jnp.maximum(m, jnp.max(peak, axis=-1, keepdims=True) * cc)
    scale = jnp.exp2(m - new)
    shift = new[:, :1]
    acc, l = acc * scale, l * scale
    for s, (k, v) in zip(scores, pieces):
        w = jnp.exp2(s * cc - shift)
        for i in range(0, s.shape[1], D):
            l = l + w[:, i:i + D]
        acc = acc + jnp.dot(w.astype(BF16), v, preferred_element_type=F32)
    return acc, l, new


class Copy:
    def __init__(self, sems, number, src, dst, device, sends=None, receives=None):
        self.args = (src, dst, sems[0].at[number], sems[1].at[number])
        self.device, self.sends, self.receives = device, sends, receives

    def act(self, name, condition):
        def go():
            getattr(pltpu.make_async_remote_copy(
                *self.args, device_id=self.device, device_id_type=MESH), name)()
        if condition is None:
            go()
        else:
            pl.when(condition)(go)

    def start(self):
        self.act("start", self.sends)

    def wait_send(self):
        self.act("wait_send", self.sends)

    def wait_recv(self):
        self.act("wait_recv", self.receives)


def main_kernel(order, place, tlen, vq, vk, vv, tq, tk, tv, qg, kg, v_out, t_out,
                q_all, kvg, rbuf, acc, tot, top, o_send, l_send, o_got, l_got, final,
                raw, raw_t, rows, tg, tf, tx, tpo, tpl, tao, tal, tb, td, te, rco, rcl, rxo, rxl, ry, rz, tr, ends,
                ssem, rsem, ret_s, ret_r):
    t = lax.axis_index("ta")
    s = lax.axis_index("sa")
    a, b, c = s // SW, s % SW, s % 2
    x, y, zh = s // 16, (s // 4) % 4, (s // 2) % 2
    z = zh * 4 + t
    even = a % 2 == 0
    has_out = jnp.where(c == 0, b > 0, b < SW - 1)
    middle, edge = (b == 3) | (b == 4), (b == 0) | (b == SW - 1)
    has_far = jnp.where(even, a >= 2, a <= 5)
    far_send = jnp.where(even, a <= 4, a >= 3)
    t_up, t_dn, r_up, r_dn = t < 3, t > 0, a < 7, a > 0
    mate = (t, s + 1 - 2 * c)
    outd = (t, s - 1 + 2 * c)
    d_tup, d_tdn, d_rup, d_rdn = (t + 1, s), (t - 1, s), (t, s + SW), (t, s - SW)
    pair = (t, jnp.where(even, s + SW, s - SW))
    fard = (t, jnp.where(even, s + 2 * SW, s - 2 * SW))
    via = (t, jnp.where(b == 3, s + 4, s - 4))
    hop = (t, jnp.where(b % 4 == 0, s + 3, s - 3))
    peers = {"x": [], "y": [], "z": []}
    for i in range(1, 4):
        x2, y2 = (x + i) % 4, (y + i) % 4
        peers["x"].append((x2, (t, s + 16 * (x2 - x))))
        peers["y"].append((y2, (t, s + 4 * (y2 - y))))
    for i in range(1, 8):
        z2 = (z + i) % 8
        peers["z"].append((z2, (z2 % 4, s + 2 * (z2 // 4 - zh))))

    bar = pltpu.get_barrier_semaphore()

    def greet(device, exists=None):
        def go():
            pl.semaphore_signal(bar, inc=1, device_id=device, device_id_type=MESH)
        if exists is None:
            go()
        else:
            pl.when(exists)(go)

    greet(mate)
    greet(outd, has_out)
    greet(hop, middle | edge)
    greet(d_tup, t_up)
    greet(d_tdn, t_dn)
    greet(d_rup, r_up)
    greet(d_rdn, r_dn)
    for axis in "xyz":
        for _, device in peers[axis]:
            greet(device)

    sems = (ssem, rsem)
    number = [0]

    def copy(src, dst, device, sends=None, receives=None):
        number[0] += 1
        return Copy(sems, number[0] - 1, src, dst, device, sends, receives)

    def both(src, dst_low, dst_high, axis):
        if axis == "t":
            return [copy(src, dst_low, d_tup, t_up, t_dn), copy(src, dst_high, d_tdn, t_dn, t_up)]
        return [copy(src, dst_low, d_rup, r_up, r_dn), copy(src, dst_high, d_rdn, r_dn, r_up)]

    def slot(first, n, piece):
        return kvg.at[pl.ds(first, n), piece]

    out_c0 = copy(slot(4, 2, 0), slot(4, 2, 2), outd, has_out, has_out)
    out_c2 = copy(slot(6, 2, 0), slot(6, 2, 2), outd, has_out, has_out)
    near = has_out & jnp.logical_not(middle)
    out_c1, via_c1, hop_c1 = (copy(slot(2, 2, 0), slot(2, 2, 2), outd, near, near),
                              copy(slot(2, 2, 0), rbuf.at[pl.ds(2, 2)], via, middle, edge),
                              copy(rbuf.at[pl.ds(2, 2)], slot(2, 2, 2), hop, edge, middle))
    out_c4, via_c4, hop_c4 = (copy(slot(0, 2, 0), slot(0, 2, 2), outd, near, near),
                              copy(slot(0, 2, 0), rbuf.at[pl.ds(0, 2)], via, middle, edge),
                              copy(rbuf.at[pl.ds(0, 2)], slot(0, 2, 2), hop, edge, middle))
    mate_kv = copy(slot(0, 8, 0), slot(0, 8, 1), mate)
    rows_pair = copy(slot(8, 4, 0), slot(8, 4, 1), pair)
    rows_far = copy(slot(8, 4, 1), slot(8, 4, 2), fard, far_send, has_far)
    own_pair = copy(slot(4, 2, 0), slot(12, 2, 0), pair)
    own_far = copy(slot(12, 2, 0), slot(14, 2, 0), fard, far_send, has_far)
    out_pair = copy(slot(4, 2, 2), slot(12, 2, 2), pair, has_out, has_out)
    out_far = copy(slot(12, 2, 2), slot(14, 2, 2), fard, far_send & has_out, has_far & has_out)
    mate_pair = copy(slot(12, 2, 0), slot(12, 2, 1), mate)
    mate_far = copy(slot(14, 2, 0), slot(14, 2, 1), mate, has_far, has_far)
    q_row = both(q_all.at[0, pl.ds(2, 2)], q_all.at[1, pl.ds(2, 2)], q_all.at[2, pl.ds(2, 2)], "r")
    q_time = both(q_all.at[0, pl.ds(4, 6)], q_all.at[1, pl.ds(4, 6)], q_all.at[2, pl.ds(4, 6)], "t")
    gi = y * 8 + z
    g_z = [copy(tg.at[gi], tg.at[gi], device) for _, device in peers["z"]]
    g_y = [copy(tg.at[pl.ds(y * 8, 8)], tg.at[pl.ds(y * 8, 8)], device) for _, device in peers["y"]]
    first, rest = pl.ds(0, HEADS), pl.ds(HEADS, 2 * HEADS)
    g_xq = [copy(tx.at[first, c, x], tx.at[first, c, x], device) for _, device in peers["x"]]
    g_xkv = [copy(tx.at[rest, c, x], tx.at[rest, c, x], device) for _, device in peers["x"]]
    g_cq = copy(tx.at[first, c], tx.at[first, c], mate)
    g_ckv = copy(tx.at[rest, c], tx.at[rest, c], mate)
    s_c = [copy(tpo.at[pl.ds(6 * (1 - c), 6)], rco, mate), copy(tpl.at[1 - c], rcl, mate)]
    s_x = [copy(tao.at[:, :, x2], rxo.at[i], device) for i, (x2, device) in enumerate(peers["x"])]
    s_x += [copy(tal.at[:, x2], rxl.at[i], device) for i, (x2, device) in enumerate(peers["x"])]
    s_y = [copy(tb.at[:, :, :, pl.ds(8 * y2, 8)], ry.at[i], device) for i, (y2, device) in enumerate(peers["y"])]
    s_z = [copy(td.at[z2], rz.at[i], device) for i, (z2, device) in enumerate(peers["z"])]
    s_e = copy(te.at[pl.ds(8 * (1 - c), 8)], tr, mate)

    def start(*items):
        for item in items:
            item.start()

    def got(*items):
        for item in items:
            item.wait_recv()

    def norm(value, gain):
        u = value.astype(F32)
        return u * lax.rsqrt(jnp.mean(u * u, axis=-1, keepdims=True) + EPS) * gain[...]

    for h in range(HEADS):
        here = pl.ds(h * D, D)
        raw_t[h] = jnp.broadcast_to(norm(tq[:, here], qg), (8, D))
        raw_t[HEADS + h] = jnp.broadcast_to(norm(tk[:, here], kg), (8, D))
        raw_t[2 * HEADS + h] = jnp.broadcast_to(tv[:, here].astype(F32), (8, D))
    for k, ref in enumerate((vk, vv, vq)):
        for h in range(HEADS):
            raw[k, h] = ref[0, 0, :, pl.ds(h * D, D)]

    def prepare_q(first, n):
        def one(p, _):
            q_all[0, p] = norm(raw[2, order[p]], qg).astype(BF16)
            return 0
        lax.fori_loop(first, first + n, one, 0)

    def prepare_kv(first, n):
        def one(p, _):
            kvg[p, 0, 0] = norm(raw[0, order[p]], kg).astype(BF16)
            kvg[p, 0, 1] = raw[1, order[p]]
            return 0
        lax.fori_loop(first, first + n, one, 0)

    def prepare_text(p, _):
        h = order[p]
        for k in range(3):
            rows[pl.ds(k * HEADS + p, 1), :] = raw_t[k * HEADS + h][:1]
        return 0

    rows[...] = jnp.zeros_like(rows)
    lax.fori_loop(0, HEADS, prepare_text, 0)
    tg[gi] = rows[...].astype(BF16)
    prepare_kv(4, 2)

    count = 14 + has_out.astype(jnp.int32) + t_up.astype(jnp.int32) + t_dn.astype(jnp.int32)
    count = count + r_up.astype(jnp.int32) + r_dn.astype(jnp.int32) + (middle | edge).astype(jnp.int32)
    pl.semaphore_wait(bar, count)

    index = lax.broadcasted_iota(jnp.int32, (1, TEXT), 1)
    i_c, i_x, i_y, i_z = index // 128, (index // 32) % 4, (index // 8) % 4, index % 8
    original = (i_z % 4) * 64 + i_x * 16 + i_y * 4 + (i_z // 4) * 2 + i_c
    text_bias = jnp.where(original < tlen[0], 0.0, -BIG).astype(F32)
    lane = lax.broadcasted_iota(jnp.int32, (1, D), 1) // 16

    def packed(l, h, old):
        return jnp.where(lane == h, l, old)

    def unpacked(l, h):
        return jnp.sum(jnp.where((lane == h) & (lax.broadcasted_iota(jnp.int32, (1, D), 1) % 16 == 0), l, 0.0),
                       axis=-1, keepdims=True)

    def text(j):
        return tx[j].reshape(TEXT, D)

    def sort_text():
        def widen(i, _):
            tf[pl.ds(pl.multiple_of(i * 8 * TROWS, 8 * TROWS), 8 * TROWS)] = (
                tg[pl.ds(i * 8, 8)].astype(F32).reshape(8 * TROWS, D))
            return 0
        lax.fori_loop(0, 4, widen, 0)

        def pick(j, _):
            tx[j, c, x] = tf[pl.ds(j, 32, stride=TROWS), :].astype(BF16)
            return 0
        lax.fori_loop(0, 3 * HEADS, pick, 0)

    def text_partial():
        for half in range(2):
            def partial(i, l_packed):
                h = half * 6 + i
                o, l = attend(text(h), [(kvg[h, 0, 0], kvg[h, 0, 1])])
                tpo[h] = o.astype(BF16).reshape(2, 4, 32, D)
                return packed(l, i, l_packed)
            tpl[half] = lax.fori_loop(0, 6, partial, jnp.zeros((TEXT, D), F32)).reshape(2, 4, 32, D)

    def reduce_c():
        def one(h, l_packed):
            o, l = merge(tpo[6 * c + h].reshape(TEXT, D).astype(F32), unpacked(tpl[c].reshape(TEXT, D), h),
                         rco[h].reshape(TEXT, D).astype(F32), unpacked(rcl[...].reshape(TEXT, D), h))
            tao[h] = o.astype(BF16).reshape(2, 4, 32, D)
            return packed(l, h, l_packed)
        tal[...] = lax.fori_loop(0, 6, one, jnp.zeros((TEXT, D), F32)).reshape(2, 4, 32, D)

    def reduce_x():
        def one(h, _):
            o, l = tao[h, :, x].reshape(64, D).astype(F32), unpacked(tal[:, x].reshape(64, D), h)
            for i in range(3):
                o, l = merge(o, l, rxo[i, h].reshape(64, D).astype(F32), unpacked(rxl[i].reshape(64, D), h))
            tb[h, 0] = o.reshape(2, 32, D)
            tb[h, 1] = jnp.broadcast_to(l, (64, D)).reshape(2, 32, D)
            return 0
        lax.fori_loop(0, 6, one, 0)

        @pl.when((y == 0) & (z == 0))
        def _():
            def self_part(h, _):
                k = 6 * c + h
                o, l = attend(tx[k, :, x].reshape(64, D), [(text(HEADS + k), text(2 * HEADS + k))], text_bias)
                o, l = merge(tb[h, 0].reshape(64, D), tb[h, 1].reshape(64, D), o, l)
                tb[h, 0] = o.reshape(2, 32, D)
                tb[h, 1] = l.reshape(2, 32, D)
                return 0
            lax.fori_loop(0, 6, self_part, 0)

    def reduce_y():
        for h in range(6):
            for cc in range(2):
                eight = pl.ds(pl.multiple_of(8 * y, 8), 8)
                o, l = tb[h, 0, cc, eight], tb[h, 1, cc, eight]
                for i in range(3):
                    o, l = merge(o, l, ry[i, h, 0, cc], ry[i, h, 1, cc])
                for k, value in enumerate((o, l)):
                    for zz in range(8):
                        td[zz, pl.ds(k * 16 + cc * 8 + h, 1), :] = value[zz:zz + 1]

    def reduce_z():
        o, l = td[z, pl.ds(0, 16)], td[z, pl.ds(16, 16)]
        for i in range(7):
            o, l = merge(o, l, rz[i, pl.ds(0, 16)], rz[i, pl.ds(16, 16)])
        te[...] = o

    def spread_out(l):
        return jnp.transpose(jnp.broadcast_to(l, (D, TOK)))

    start(*g_z)
    prepare_q(4, 6)
    got(*g_z)
    start(*g_y)
    prepare_kv(8, 4)
    prepare_kv(6, 2)
    got(*g_y)
    sort_text()
    start(*g_xq)
    start(out_c0, own_pair, *q_time)
    start(rows_pair, out_c2)
    prepare_kv(2, 2)
    start(out_c1, via_c1)
    prepare_kv(0, 2)
    start(mate_kv, out_c4, via_c4, *g_xkv)
    prepare_q(2, 2)
    start(*q_row)
    prepare_q(0, 2)
    prepare_q(10, 2)

    def return_copies(h, d):
        row = h < 4
        dev_t = jnp.where(row, t, t - 1 + 2 * d)
        dev_s = jnp.where(row, s + (2 * d - 1) * SW, s)
        device = (dev_t, dev_s)
        return [
            pltpu.make_async_remote_copy(src_ref=o_send.at[d, h - 2], dst_ref=o_got.at[1 - d, h - 2],
                                         send_sem=ret_s.at[0, d, h - 2], recv_sem=ret_r.at[0, 1 - d, h - 2],
                                         device_id=device, device_id_type=MESH),
            pltpu.make_async_remote_copy(src_ref=l_send.at[d, h - 2], dst_ref=l_got.at[1 - d, h - 2],
                                         send_sem=ret_s.at[1, d, h - 2], recv_sem=ret_r.at[1, 1 - d, h - 2],
                                         device_id=device, device_id_type=MESH),
        ]

    def there(h, d):
        row = h < 4
        low = jnp.where(row, a, t) > 0
        high = jnp.where(row, a - 4, t) < 3
        return (h >= 2) & (h < 10) & jnp.where(d == 0, low, high)

    def reset(i, _):
        for ref, value in ((acc, 0.0), (tot, 0.0), (top, -BIG)):
            ref[i // HEADS, i % HEADS] = jnp.full((TOK, D), value, F32)
        return 0

    lax.fori_loop(0, 3 * HEADS, reset, 0)

    def take(h, n, pieces, bias=None):
        refs = (acc, tot, top)
        state = [ref[:n, h].reshape(n * TOK, D) for ref in refs]
        for ref, value in zip(refs, absorb(q_all[:n, h].reshape(n * TOK, D), pieces, state, bias)):
            ref[:n, h] = value.reshape(n, TOK, D)

    segments = [
        (3, 8, 2, 0, 1, lambda: (
            got(*g_xq), start(g_cq), got(own_pair), start(own_far, mate_pair), got(g_cq), text_partial(), start(*s_c),
            got(rows_pair), start(rows_far), got(*s_c), reduce_c(), start(*s_x), got(rows_far, *q_time))),
        (1, 10, 2, 0, 0, lambda: (got(*g_xkv), start(g_ckv), got(own_far), start(mate_far))),
        (0, 0, 12, 0, 0, lambda: (got(via_c1), start(hop_c1), got(g_ckv), got(*s_x), reduce_x(), start(*s_y))),
        (3, 4, 2, 0, 0, lambda: (got(out_c0), start(out_pair), got(mate_kv))),
        (3, 4, 2, 1, 0, lambda: (got(via_c4), start(hop_c4), got(mate_pair, out_pair), start(out_far), got(*s_y), reduce_y(), start(*s_z))),
        (3, 6, 2, 0, 1, lambda: (got(out_c2),)),
        (3, 4, 2, 2, 1, lambda: (got(mate_far, out_far), got(*s_z), reduce_z(), start(s_e))),
        (3, 2, 2, 0, 1, lambda: (got(out_c1, hop_c1, *q_row))),
        (1, 0, 2, 0, 0, lambda: got(out_c4, hop_c4)),
    ]

    def pick_of(n, field):
        value = segments[0][field]
        for i in range(1, len(segments)):
            if segments[i][field] != segments[i - 1][field]:
                value = jnp.where(n >= i, segments[i][field], value)
        return value

    def segment(n, _):
        for i, item in enumerate(segments):
            pl.when(n == i)(functools.partial(lambda event: event() and None, item[5]))
        kind, h0, nh, g, back = (pick_of(n, field) for field in range(5))
        present = (g < 2) | has_far

        def work(i, _):
            h = h0 + i
            group = h + jnp.where(g == 0, 0, 6 + 2 * g)
            late = jnp.where(h < 8, has_out, has_far)
            pieces = [(kvg.at[group, j, 0], kvg.at[group, j, 1]) for j in range(3)]

            def read(count):
                return [(k[...], v[...]) for k, v in pieces[:count]]

            for n_q in (3, 1):
                @pl.when((kind == n_q) & present & late)
                def _():
                    take(h, n_q, read(3))

                @pl.when((kind == n_q) & present & jnp.logical_not(late))
                def _():
                    take(h, n_q, read(2))

            @pl.when(kind == 0)
            def _():
                take(h, 1, [(text(HEADS + h), text(2 * HEADS + h))], text_bias)

            for d in range(2):
                @pl.when((back == 1) & there(h, d))
                def _():
                    total = jnp.sum(tot[d + 1, h], axis=-1, keepdims=True)
                    o_send[d, h - 2] = (acc[d + 1, h] / total).astype(BF16)
                    l_send[d, h - 2] = jnp.transpose(top[d + 1, h] + jnp.log2(total))[:8]
                    for item in return_copies(h, d):
                        item.start()
            return 0

        lax.fori_loop(0, nh, work, 0)
        return 0

    lax.fori_loop(0, len(segments), segment, 0)

    def finish(n, _):
        duo = n // 2
        h = jnp.where(duo == 0, 0, jnp.where(duo == 1, 10, jnp.where(duo == 2, 8, jnp.where(
            duo == 3, 6, jnp.where(duo == 4, 4, 2))))) + n % 2
        for d in range(2):
            @pl.when(there(h, d))
            def _():
                for item in return_copies(h, 1 - d):
                    item.wait_recv()
                theirs = spread_out(l_got[d, h - 2][:1])
                mine = top[0, h]
                new = jnp.maximum(mine, theirs)
                w1, w2 = jnp.exp2(mine - new), jnp.exp2(theirs - new)
                acc[0, h] = acc[0, h] * w1 + o_got[d, h - 2].astype(F32) * w2
                tot[0, h] = tot[0, h] * w1 + w2 * (1.0 / D)
                top[0, h] = new
                for item in return_copies(h, d):
                    item.wait_send()
        final[h] = (acc[0, h] / jnp.sum(tot[0, h], axis=-1, keepdims=True)).astype(BF16)
        return 0

    lax.fori_loop(0, HEADS, finish, 0)

    got(s_e)
    mine = te[pl.ds(pl.multiple_of(8 * c, 8), 8), :]
    for i in range(6):
        ends[6 * c + i] = jnp.broadcast_to(mine[i:i + 1], (8, D))
        ends[6 * (1 - c) + i] = jnp.broadcast_to(tr[i:i + 1, :], (8, D))
    for h in range(HEADS):
        p = place[h]
        here = pl.ds(h * D, D)
        v_out[0, 0, :, here] = final[p]
        t_out[:, here] = ends[p][:1].astype(BF16)
    for item in ([out_c0, out_c1, out_c2, out_c4, via_c1, via_c4, hop_c1, hop_c4, mate_kv, rows_pair, rows_far, own_pair,
                  own_far, out_pair, out_far, mate_pair, mate_far, g_cq, g_ckv, s_e]
                 + q_row + q_time + g_z + g_y + g_xq + g_xkv + s_c + s_x + s_y + s_z):
        item.wait_send()


N_COPIES = 64


def main_call(order, place, text_len, arrays):
    shapes = [
        pltpu.VMEM((3, HEADS, TOK, D), BF16),
        pltpu.VMEM((16, 3, 2, TOK, D), BF16),
        pltpu.VMEM((4, 2, TOK, D), BF16),
        pltpu.VMEM((3, HEADS, TOK, D), F32),
        pltpu.VMEM((3, HEADS, TOK, D), F32),
        pltpu.VMEM((3, HEADS, TOK, D), F32),
        pltpu.VMEM((2, 8, TOK, D), BF16),
        pltpu.VMEM((2, 8, 8, TOK), F32),
        pltpu.VMEM((2, 8, TOK, D), BF16),
        pltpu.VMEM((2, 8, 8, TOK), F32),
        pltpu.VMEM((HEADS, TOK, D), BF16),
        pltpu.VMEM((3, HEADS, TOK, D), BF16),
        pltpu.VMEM((3 * HEADS, 8, D), F32),
        pltpu.VMEM((TROWS, D), F32),
        pltpu.VMEM((32, TROWS, D), BF16),
        pltpu.VMEM((32 * TROWS, D), F32),
        pltpu.VMEM((3 * HEADS, 2, 4, 32, D), BF16),
        pltpu.VMEM((HEADS, 2, 4, 32, D), BF16),
        pltpu.VMEM((2, 2, 4, 32, D), F32),
        pltpu.VMEM((6, 2, 4, 32, D), BF16),
        pltpu.VMEM((2, 4, 32, D), F32),
        pltpu.VMEM((6, 2, 2, 32, D), F32),
        pltpu.VMEM((8, 32, D), F32),
        pltpu.VMEM((16, D), F32),
        pltpu.VMEM((6, 2, 4, 32, D), BF16),
        pltpu.VMEM((2, 4, 32, D), F32),
        pltpu.VMEM((3, 6, 2, 32, D), BF16),
        pltpu.VMEM((3, 2, 32, D), F32),
        pltpu.VMEM((3, 6, 2, 2, 8, D), F32),
        pltpu.VMEM((7, 32, D), F32),
        pltpu.VMEM((8, D), F32),
        pltpu.VMEM((HEADS, 8, D), F32),
        pltpu.SemaphoreType.DMA((N_COPIES,)),
        pltpu.SemaphoreType.DMA((N_COPIES,)),
        pltpu.SemaphoreType.DMA((2, 2, 8)),
        pltpu.SemaphoreType.DMA((2, 2, 8)),
    ]
    scalars, vmem = pl.BlockSpec(memory_space=pltpu.SMEM), pl.BlockSpec(memory_space=pltpu.VMEM)
    return pl.pallas_call(
        main_kernel,
        out_shape=(jax.ShapeDtypeStruct(arrays[0].shape, BF16), jax.ShapeDtypeStruct(arrays[3].shape, BF16)),
        in_specs=[scalars] * 3 + [vmem] * 8,
        out_specs=(vmem, vmem),
        scratch_shapes=shapes,
        compiler_params=pltpu.CompilerParams(
            collective_id=0, has_side_effects=True, vmem_limit_bytes=VMEM_LIMIT),
        name="tiles",
    )(order, place, text_len, *arrays)


def local(video_q, video_k, video_v, text_q, text_k, text_v, q_gain, k_gain, text_len, window):
    wide = (window == 3).astype(jnp.int32)
    code = wide[:, 0] * 4 + wide[:, 1] * 2 + wide[:, 2]
    rank = jnp.zeros_like(code)
    for value, place in enumerate(RANK_OF_CODE):
        rank = jnp.where(code == value, place, rank)
    key = rank * HEADS + jnp.arange(HEADS, dtype=jnp.int32)
    position = jnp.sum((key[None, :] < key[:, None]).astype(jnp.int32), axis=1)
    places = jnp.arange(HEADS, dtype=jnp.int32)
    order = jnp.sum(jnp.where(position[None, :] == places[:, None], places[None, :], 0), axis=1)

    return main_call(order, position, text_len, (
        video_q, video_k, video_v, text_q, text_k, text_v, q_gain[None], k_gain[None]))


def solution(mesh):
    tiles, rows = P("ta", "sa", None, None), P(("ta", "sa"), None)
    return jax.shard_map(
        local, mesh=mesh,
        in_specs=(tiles, tiles, tiles, rows, rows, rows, P(), P(), P(), P()),
        out_specs=(tiles, rows),
        check_vma=False,
    )
```

```python
import functools
import math

import jax
import jax.numpy as jnp
from jax import lax
from jax.experimental import pallas as pl
from jax.experimental.pallas import tpu as pltpu
from jax.sharding import PartitionSpec as P

MESH = pl.DeviceIdType.MESH
EPS = 1e-6
F32, BF16 = jnp.float32, jnp.bfloat16
HEADS, D, TOK, TEXT = 12, 128, 384, 256
SW = 8
BIG = 1e30
TROWS = 48
VMEM_LIMIT = 61 * 2**20
RANK_OF_CODE = (0, 0, 5, 1, 0, 3, 4, 2)


def merge(o1, l1, o2, l2):
    top = jnp.maximum(l1, l2)
    w1 = jnp.exp2(l1 - top)
    w2 = jnp.exp2(l2 - top)
    total = w1 + w2
    return (o1 * w1 + o2 * w2) / total, top + jnp.log2(total)


def dot_t(a, b):
    return lax.dot_general(a, b, (((1,), (1,)), ((), ())), preferred_element_type=F32)


def attend(q, pieces, bias=None):
    cc = math.log2(math.e) / math.sqrt(D)
    scores, peak = [], None
    for k, v in pieces:
        s = dot_t(q, k)
        if bias is not None:
            s = s + bias
        scores.append(s)
        row = jnp.max(s, axis=-1, keepdims=True)
        peak = row if peak is None else jnp.maximum(peak, row)
    peak = peak * cc
    total = None
    for s, (k, v) in zip(scores, pieces):
        w = jnp.exp2(s * cc - peak).astype(BF16)
        part = jnp.dot(w, jnp.concatenate([v, jnp.ones(v.shape, BF16)], axis=1), preferred_element_type=F32)
        total = part if total is None else total + part
    o, l = total[:, :D], total[:, D:]
    return o / l, peak + jnp.log2(l)


def absorb(q, pieces, state, bias=None):
    cc = math.log2(math.e) / math.sqrt(D)
    acc, l, m = state
    scores, peak = [], None
    for k, v in pieces:
        s = dot_t(q, k)
        if bias is not None:
            s = s + bias
        scores.append(s)
        for i in range(0, s.shape[1], D):
            part = s[:, i:i + D]
            peak = part if peak is None else jnp.maximum(peak, part)
    new = jnp.maximum(m, jnp.max(peak, axis=-1, keepdims=True) * cc)
    scale = jnp.exp2(m - new)
    shift = new[:, :1]
    acc, l = acc * scale, l * scale
    for s, (k, v) in zip(scores, pieces):
        w = jnp.exp2(s * cc - shift)
        for i in range(0, s.shape[1], D):
            l = l + w[:, i:i + D]
        acc = acc + jnp.dot(w.astype(BF16), v, preferred_element_type=F32)
    return acc, l, new


class Copy:
    def __init__(self, sems, number, src, dst, device, sends=None, receives=None):
        self.args = (src, dst, sems[0].at[number], sems[1].at[number])
        self.device, self.sends, self.receives = device, sends, receives

    def act(self, name, condition):
        def go():
            getattr(pltpu.make_async_remote_copy(
                *self.args, device_id=self.device, device_id_type=MESH), name)()
        if condition is None:
            go()
        else:
            pl.when(condition)(go)

    def start(self):
        self.act("start", self.sends)

    def wait_send(self):
        self.act("wait_send", self.sends)

    def wait_recv(self):
        self.act("wait_recv", self.receives)


def main_kernel(order, place, tlen, vq, vk, vv, tq, tk, tv, qg, kg, v_out, t_out,
                q_all, kvg, rbuf, acc, tot, top, o_send, l_send, o_got, l_got, final,
                raw, raw_t, rows, tg, tf, tx, tpo, tpl, tao, tal, tb, td, te, rco, rcl, rxo, rxl, ry, rz, tr, ends,
                ssem, rsem, ret_s, ret_r):
    t = lax.axis_index("ta")
    s = lax.axis_index("sa")
    a, b, c = s // SW, s % SW, s % 2
    x, y, zh = s // 16, (s // 4) % 4, (s // 2) % 2
    z = zh * 4 + t
    even = a % 2 == 0
    has_out = jnp.where(c == 0, b > 0, b < SW - 1)
    middle, edge = (b == 3) | (b == 4), (b == 0) | (b == SW - 1)
    has_far = jnp.where(even, a >= 2, a <= 5)
    far_send = jnp.where(even, a <= 4, a >= 3)
    t_up, t_dn, r_up, r_dn = t < 3, t > 0, a < 7, a > 0
    mate = (t, s + 1 - 2 * c)
    outd = (t, s - 1 + 2 * c)
    d_tup, d_tdn, d_rup, d_rdn = (t + 1, s), (t - 1, s), (t, s + SW), (t, s - SW)
    pair = (t, jnp.where(even, s + SW, s - SW))
    fard = (t, jnp.where(even, s + 2 * SW, s - 2 * SW))
    via = (t, jnp.where(b == 3, s + 4, s - 4))
    hop = (t, jnp.where(b % 4 == 0, s + 3, s - 3))
    peers = {"x": [], "y": [], "z": []}
    for i in range(1, 4):
        x2, y2 = (x + i) % 4, (y + i) % 4
        peers["x"].append((x2, (t, s + 16 * (x2 - x))))
        peers["y"].append((y2, (t, s + 4 * (y2 - y))))
    for i in range(1, 8):
        z2 = (z + i) % 8
        peers["z"].append((z2, (z2 % 4, s + 2 * (z2 // 4 - zh))))

    bar = pltpu.get_barrier_semaphore()

    def greet(device, exists=None):
        def go():
            pl.semaphore_signal(bar, inc=1, device_id=device, device_id_type=MESH)
        if exists is None:
            go()
        else:
            pl.when(exists)(go)

    greet(mate)
    greet(outd, has_out)
    greet(hop, middle | edge)
    greet(d_tup, t_up)
    greet(d_tdn, t_dn)
    greet(d_rup, r_up)
    greet(d_rdn, r_dn)
    for axis in "xyz":
        for _, device in peers[axis]:
            greet(device)

    sems = (ssem, rsem)
    number = [0]

    def copy(src, dst, device, sends=None, receives=None):
        number[0] += 1
        return Copy(sems, number[0] - 1, src, dst, device, sends, receives)

    def both(src, dst_low, dst_high, axis):
        if axis == "t":
            return [copy(src, dst_low, d_tup, t_up, t_dn), copy(src, dst_high, d_tdn, t_dn, t_up)]
        return [copy(src, dst_low, d_rup, r_up, r_dn), copy(src, dst_high, d_rdn, r_dn, r_up)]

    def slot(first, n, piece):
        return kvg.at[pl.ds(first, n), piece]

    out_c0 = copy(slot(4, 2, 0), slot(4, 2, 2), outd, has_out, has_out)
    out_c2 = copy(slot(6, 2, 0), slot(6, 2, 2), outd, has_out, has_out)
    near = has_out & jnp.logical_not(middle)
    out_c1, via_c1, hop_c1 = (copy(slot(2, 2, 0), slot(2, 2, 2), outd, near, near),
                              copy(slot(2, 2, 0), rbuf.at[pl.ds(2, 2)], via, middle, edge),
                              copy(rbuf.at[pl.ds(2, 2)], slot(2, 2, 2), hop, edge, middle))
    out_c4, via_c4, hop_c4 = (copy(slot(0, 2, 0), slot(0, 2, 2), outd, near, near),
                              copy(slot(0, 2, 0), rbuf.at[pl.ds(0, 2)], via, middle, edge),
                              copy(rbuf.at[pl.ds(0, 2)], slot(0, 2, 2), hop, edge, middle))
    mate_kv = copy(slot(0, 8, 0), slot(0, 8, 1), mate)
    rows_pair = copy(slot(8, 4, 0), slot(8, 4, 1), pair)
    rows_far = copy(slot(8, 4, 1), slot(8, 4, 2), fard, far_send, has_far)
    own_pair = copy(slot(4, 2, 0), slot(12, 2, 0), pair)
    own_far = copy(slot(12, 2, 0), slot(14, 2, 0), fard, far_send, has_far)
    out_pair = copy(slot(4, 2, 2), slot(12, 2, 2), pair, has_out, has_out)
    out_far = copy(slot(12, 2, 2), slot(14, 2, 2), fard, far_send & has_out, has_far & has_out)
    mate_pair = copy(slot(12, 2, 0), slot(12, 2, 1), mate)
    mate_far = copy(slot(14, 2, 0), slot(14, 2, 1), mate, has_far, has_far)
    q_row = both(q_all.at[0, pl.ds(2, 2)], q_all.at[1, pl.ds(2, 2)], q_all.at[2, pl.ds(2, 2)], "r")
    q_time = both(q_all.at[0, pl.ds(4, 6)], q_all.at[1, pl.ds(4, 6)], q_all.at[2, pl.ds(4, 6)], "t")
    gi = y * 8 + z
    g_z = [copy(tg.at[gi], tg.at[gi], device) for _, device in peers["z"]]
    g_y = [copy(tg.at[pl.ds(y * 8, 8)], tg.at[pl.ds(y * 8, 8)], device) for _, device in peers["y"]]
    first, rest = pl.ds(0, HEADS), pl.ds(HEADS, 2 * HEADS)
    g_xq = [copy(tx.at[first, c, x], tx.at[first, c, x], device) for _, device in peers["x"]]
    g_xkv = [copy(tx.at[rest, c, x], tx.at[rest, c, x], device) for _, device in peers["x"]]
    g_cq = copy(tx.at[first, c], tx.at[first, c], mate)
    g_ckv = copy(tx.at[rest, c], tx.at[rest, c], mate)
    s_c = [copy(tpo.at[pl.ds(6 * (1 - c), 6)], rco, mate), copy(tpl.at[1 - c], rcl, mate)]
    s_x = [copy(tao.at[:, :, x2], rxo.at[i], device) for i, (x2, device) in enumerate(peers["x"])]
    s_x += [copy(tal.at[:, x2], rxl.at[i], device) for i, (x2, device) in enumerate(peers["x"])]
    s_y = [copy(tb.at[:, :, :, pl.ds(8 * y2, 8)], ry.at[i], device) for i, (y2, device) in enumerate(peers["y"])]
    s_z = [copy(td.at[z2], rz.at[i], device) for i, (z2, device) in enumerate(peers["z"])]
    s_e = copy(te.at[pl.ds(8 * (1 - c), 8)], tr, mate)

    def start(*items):
        for item in items:
            item.start()

    def got(*items):
        for item in items:
            item.wait_recv()

    def norm(value, gain):
        u = value.astype(F32)
        return u * lax.rsqrt(jnp.mean(u * u, axis=-1, keepdims=True) + EPS) * gain[...]

    for h in range(HEADS):
        here = pl.ds(h * D, D)
        raw_t[h] = jnp.broadcast_to(norm(tq[:, here], qg), (8, D))
        raw_t[HEADS + h] = jnp.broadcast_to(norm(tk[:, here], kg), (8, D))
        raw_t[2 * HEADS + h] = jnp.broadcast_to(tv[:, here].astype(F32), (8, D))
    for k, ref in enumerate((vk, vv, vq)):
        for h in range(HEADS):
            raw[k, h] = ref[0, 0, :, pl.ds(h * D, D)]

    def prepare_q(first, n):
        def one(p, _):
            q_all[0, p] = norm(raw[2, order[p]], qg).astype(BF16)
            return 0
        lax.fori_loop(first, first + n, one, 0)

    def prepare_kv(first, n):
        def one(p, _):
            kvg[p, 0, 0] = norm(raw[0, order[p]], kg).astype(BF16)
            kvg[p, 0, 1] = raw[1, order[p]]
            return 0
        lax.fori_loop(first, first + n, one, 0)

    def prepare_text(p, _):
        h = order[p]
        for k in range(3):
            rows[pl.ds(k * HEADS + p, 1), :] = raw_t[k * HEADS + h][:1]
        return 0

    rows[...] = jnp.zeros_like(rows)
    lax.fori_loop(0, HEADS, prepare_text, 0)
    tg[gi] = rows[...].astype(BF16)
    prepare_kv(4, 2)

    count = 14 + has_out.astype(jnp.int32) + t_up.astype(jnp.int32) + t_dn.astype(jnp.int32)
    count = count + r_up.astype(jnp.int32) + r_dn.astype(jnp.int32) + (middle | edge).astype(jnp.int32)
    pl.semaphore_wait(bar, count)

    index = lax.broadcasted_iota(jnp.int32, (1, TEXT), 1)
    i_c, i_x, i_y, i_z = index // 128, (index // 32) % 4, (index // 8) % 4, index % 8
    original = (i_z % 4) * 64 + i_x * 16 + i_y * 4 + (i_z // 4) * 2 + i_c
    text_bias = jnp.where(original < tlen[0], 0.0, -BIG).astype(F32)
    lane = lax.broadcasted_iota(jnp.int32, (1, D), 1) // 16

    def packed(l, h, old):
        return jnp.where(lane == h, l, old)

    def unpacked(l, h):
        return jnp.sum(jnp.where((lane == h) & (lax.broadcasted_iota(jnp.int32, (1, D), 1) % 16 == 0), l, 0.0),
                       axis=-1, keepdims=True)

    def text(j):
        return tx[j].reshape(TEXT, D)

    def sort_text():
        def widen(i, _):
            tf[pl.ds(pl.multiple_of(i * 8 * TROWS, 8 * TROWS), 8 * TROWS)] = (
                tg[pl.ds(i * 8, 8)].astype(F32).reshape(8 * TROWS, D))
            return 0
        lax.fori_loop(0, 4, widen, 0)

        def pick(j, _):
            tx[j, c, x] = tf[pl.ds(j, 32, stride=TROWS), :].astype(BF16)
            return 0
        lax.fori_loop(0, 3 * HEADS, pick, 0)

    def text_partial():
        for half in range(2):
            def partial(i, l_packed):
                h = half * 6 + i
                o, l = attend(text(h), [(kvg[h, 0, 0], kvg[h, 0, 1])])
                tpo[h] = o.astype(BF16).reshape(2, 4, 32, D)
                return packed(l, i, l_packed)
            tpl[half] = lax.fori_loop(0, 6, partial, jnp.zeros((TEXT, D), F32)).reshape(2, 4, 32, D)

    def reduce_c():
        def one(h, l_packed):
            o, l = merge(tpo[6 * c + h].reshape(TEXT, D).astype(F32), unpacked(tpl[c].reshape(TEXT, D), h),
                         rco[h].reshape(TEXT, D).astype(F32), unpacked(rcl[...].reshape(TEXT, D), h))
            tao[h] = o.astype(BF16).reshape(2, 4, 32, D)
            return packed(l, h, l_packed)
        tal[...] = lax.fori_loop(0, 6, one, jnp.zeros((TEXT, D), F32)).reshape(2, 4, 32, D)

    def reduce_x():
        def one(h, _):
            o, l = tao[h, :, x].reshape(64, D).astype(F32), unpacked(tal[:, x].reshape(64, D), h)
            for i in range(3):
                o, l = merge(o, l, rxo[i, h].reshape(64, D).astype(F32), unpacked(rxl[i].reshape(64, D), h))
            tb[h, 0] = o.reshape(2, 32, D)
            tb[h, 1] = jnp.broadcast_to(l, (64, D)).reshape(2, 32, D)
            return 0
        lax.fori_loop(0, 6, one, 0)

        @pl.when((y == 0) & (z == 0))
        def _():
            def self_part(h, _):
                k = 6 * c + h
                o, l = attend(tx[k, :, x].reshape(64, D), [(text(HEADS + k), text(2 * HEADS + k))], text_bias)
                o, l = merge(tb[h, 0].reshape(64, D), tb[h, 1].reshape(64, D), o, l)
                tb[h, 0] = o.reshape(2, 32, D)
                tb[h, 1] = l.reshape(2, 32, D)
                return 0
            lax.fori_loop(0, 6, self_part, 0)

    def reduce_y():
        for h in range(6):
            for cc in range(2):
                eight = pl.ds(pl.multiple_of(8 * y, 8), 8)
                o, l = tb[h, 0, cc, eight], tb[h, 1, cc, eight]
                for i in range(3):
                    o, l = merge(o, l, ry[i, h, 0, cc], ry[i, h, 1, cc])
                for k, value in enumerate((o, l)):
                    for zz in range(8):
                        td[zz, pl.ds(k * 16 + cc * 8 + h, 1), :] = value[zz:zz + 1]

    def reduce_z():
        o, l = td[z, pl.ds(0, 16)], td[z, pl.ds(16, 16)]
        for i in range(7):
            o, l = merge(o, l, rz[i, pl.ds(0, 16)], rz[i, pl.ds(16, 16)])
        te[...] = o

    def spread_out(l):
        return jnp.transpose(jnp.broadcast_to(l, (D, TOK)))

    start(*g_z)
    prepare_q(4, 6)
    got(*g_z)
    start(*g_y)
    prepare_kv(8, 4)
    prepare_kv(6, 2)
    got(*g_y)
    sort_text()
    start(*g_xq)
    start(out_c0, own_pair, *q_time)
    start(rows_pair, out_c2)
    prepare_kv(2, 2)
    start(out_c1, via_c1)
    prepare_kv(0, 2)
    start(mate_kv, out_c4, via_c4, *g_xkv)
    prepare_q(2, 2)
    start(*q_row)
    prepare_q(0, 2)
    prepare_q(10, 2)

    def return_copies(h, d):
        row = h < 4
        dev_t = jnp.where(row, t, t - 1 + 2 * d)
        dev_s = jnp.where(row, s + (2 * d - 1) * SW, s)
        device = (dev_t, dev_s)
        return [
            pltpu.make_async_remote_copy(src_ref=o_send.at[d, h - 2], dst_ref=o_got.at[1 - d, h - 2],
                                         send_sem=ret_s.at[0, d, h - 2], recv_sem=ret_r.at[0, 1 - d, h - 2],
                                         device_id=device, device_id_type=MESH),
            pltpu.make_async_remote_copy(src_ref=l_send.at[d, h - 2], dst_ref=l_got.at[1 - d, h - 2],
                                         send_sem=ret_s.at[1, d, h - 2], recv_sem=ret_r.at[1, 1 - d, h - 2],
                                         device_id=device, device_id_type=MESH),
        ]

    def there(h, d):
        row = h < 4
        low = jnp.where(row, a, t) > 0
        high = jnp.where(row, a - 4, t) < 3
        return (h >= 2) & (h < 10) & jnp.where(d == 0, low, high)

    def reset(i, _):
        for ref, value in ((acc, 0.0), (tot, 0.0), (top, -BIG)):
            ref[i // HEADS, i % HEADS] = jnp.full((TOK, D), value, F32)
        return 0

    lax.fori_loop(0, 3 * HEADS, reset, 0)

    def take(h, n, pieces, bias=None):
        refs = (acc, tot, top)
        state = [ref[:n, h].reshape(n * TOK, D) for ref in refs]
        for ref, value in zip(refs, absorb(q_all[:n, h].reshape(n * TOK, D), pieces, state, bias)):
            ref[:n, h] = value.reshape(n, TOK, D)

    segments = [
        (3, 8, 2, 0, 1, lambda: (
            got(*g_xq), start(g_cq), got(own_pair), start(own_far, mate_pair), got(g_cq), text_partial(), start(*s_c),
            got(rows_pair), start(rows_far), got(*s_c), reduce_c(), start(*s_x), got(rows_far, *q_time))),
        (1, 10, 2, 0, 0, lambda: (got(*g_xkv), start(g_ckv), got(own_far), start(mate_far))),
        (3, 4, 2, 0, 0, lambda: (got(out_c0), start(out_pair), got(mate_kv), got(via_c1), start(hop_c1))),
        (0, 0, 12, 0, 0, lambda: (got(g_ckv), got(*s_x), reduce_x(), start(*s_y))),
        (3, 4, 2, 1, 0, lambda: (got(via_c4), start(hop_c4), got(mate_pair, out_pair), start(out_far), got(*s_y), reduce_y(), start(*s_z))),
        (3, 6, 2, 0, 1, lambda: (got(out_c2),)),
        (3, 2, 2, 0, 1, lambda: (got(out_c1, hop_c1, *q_row))),
        (3, 4, 2, 2, 1, lambda: (got(mate_far, out_far), got(*s_z), reduce_z(), start(s_e))),
        (1, 0, 2, 0, 0, lambda: got(out_c4, hop_c4)),
    ]

    def pick_of(n, field):
        value = segments[0][field]
        for i in range(1, len(segments)):
            if segments[i][field] != segments[i - 1][field]:
                value = jnp.where(n >= i, segments[i][field], value)
        return value

    def segment(n, _):
        for i, item in enumerate(segments):
            pl.when(n == i)(functools.partial(lambda event: event() and None, item[5]))
        kind, h0, nh, g, back = (pick_of(n, field) for field in range(5))
        present = (g < 2) | has_far

        def work(i, _):
            h = h0 + i
            group = h + jnp.where(g == 0, 0, 6 + 2 * g)
            late = jnp.where(h < 8, has_out, has_far)
            pieces = [(kvg.at[group, j, 0], kvg.at[group, j, 1]) for j in range(3)]

            def read(count):
                return [(k[...], v[...]) for k, v in pieces[:count]]

            for n_q in (3, 1):
                @pl.when((kind == n_q) & present & late)
                def _():
                    take(h, n_q, read(3))

                @pl.when((kind == n_q) & present & jnp.logical_not(late))
                def _():
                    take(h, n_q, read(2))

            @pl.when(kind == 0)
            def _():
                take(h, 1, [(text(HEADS + h), text(2 * HEADS + h))], text_bias)

            for d in range(2):
                @pl.when((back == 1) & there(h, d))
                def _():
                    total = jnp.sum(tot[d + 1, h], axis=-1, keepdims=True)
                    o_send[d, h - 2] = (acc[d + 1, h] / total).astype(BF16)
                    l_send[d, h - 2] = jnp.transpose(top[d + 1, h] + jnp.log2(total))[:8]
                    for item in return_copies(h, d):
                        item.start()
            return 0

        lax.fori_loop(0, nh, work, 0)
        return 0

    lax.fori_loop(0, len(segments), segment, 0)

    def finish(n, _):
        duo = n // 2
        h = jnp.where(duo == 0, 0, jnp.where(duo == 1, 10, jnp.where(duo == 2, 8, jnp.where(
            duo == 3, 6, jnp.where(duo == 4, 2, 4))))) + n % 2
        for d in range(2):
            @pl.when(there(h, d))
            def _():
                for item in return_copies(h, 1 - d):
                    item.wait_recv()
                theirs = spread_out(l_got[d, h - 2][:1])
                mine = top[0, h]
                new = jnp.maximum(mine, theirs)
                w1, w2 = jnp.exp2(mine - new), jnp.exp2(theirs - new)
                acc[0, h] = acc[0, h] * w1 + o_got[d, h - 2].astype(F32) * w2
                tot[0, h] = tot[0, h] * w1 + w2 * (1.0 / D)
                top[0, h] = new
                for item in return_copies(h, d):
                    item.wait_send()
        final[h] = (acc[0, h] / jnp.sum(tot[0, h], axis=-1, keepdims=True)).astype(BF16)
        return 0

    lax.fori_loop(0, HEADS, finish, 0)

    got(s_e)
    mine = te[pl.ds(pl.multiple_of(8 * c, 8), 8), :]
    for i in range(6):
        ends[6 * c + i] = jnp.broadcast_to(mine[i:i + 1], (8, D))
        ends[6 * (1 - c) + i] = jnp.broadcast_to(tr[i:i + 1, :], (8, D))
    for h in range(HEADS):
        p = place[h]
        here = pl.ds(h * D, D)
        v_out[0, 0, :, here] = final[p]
        t_out[:, here] = ends[p][:1].astype(BF16)
    for item in ([out_c0, out_c1, out_c2, out_c4, via_c1, via_c4, hop_c1, hop_c4, mate_kv, rows_pair, rows_far, own_pair,
                  own_far, out_pair, out_far, mate_pair, mate_far, g_cq, g_ckv, s_e]
                 + q_row + q_time + g_z + g_y + g_xq + g_xkv + s_c + s_x + s_y + s_z):
        item.wait_send()


N_COPIES = 64


def main_call(order, place, text_len, arrays):
    shapes = [
        pltpu.VMEM((3, HEADS, TOK, D), BF16),
        pltpu.VMEM((16, 3, 2, TOK, D), BF16),
        pltpu.VMEM((4, 2, TOK, D), BF16),
        pltpu.VMEM((3, HEADS, TOK, D), F32),
        pltpu.VMEM((3, HEADS, TOK, D), F32),
        pltpu.VMEM((3, HEADS, TOK, D), F32),
        pltpu.VMEM((2, 8, TOK, D), BF16),
        pltpu.VMEM((2, 8, 8, TOK), F32),
        pltpu.VMEM((2, 8, TOK, D), BF16),
        pltpu.VMEM((2, 8, 8, TOK), F32),
        pltpu.VMEM((HEADS, TOK, D), BF16),
        pltpu.VMEM((3, HEADS, TOK, D), BF16),
        pltpu.VMEM((3 * HEADS, 8, D), F32),
        pltpu.VMEM((TROWS, D), F32),
        pltpu.VMEM((32, TROWS, D), BF16),
        pltpu.VMEM((32 * TROWS, D), F32),
        pltpu.VMEM((3 * HEADS, 2, 4, 32, D), BF16),
        pltpu.VMEM((HEADS, 2, 4, 32, D), BF16),
        pltpu.VMEM((2, 2, 4, 32, D), F32),
        pltpu.VMEM((6, 2, 4, 32, D), BF16),
        pltpu.VMEM((2, 4, 32, D), F32),
        pltpu.VMEM((6, 2, 2, 32, D), F32),
        pltpu.VMEM((8, 32, D), F32),
        pltpu.VMEM((16, D), F32),
        pltpu.VMEM((6, 2, 4, 32, D), BF16),
        pltpu.VMEM((2, 4, 32, D), F32),
        pltpu.VMEM((3, 6, 2, 32, D), BF16),
        pltpu.VMEM((3, 2, 32, D), F32),
        pltpu.VMEM((3, 6, 2, 2, 8, D), F32),
        pltpu.VMEM((7, 32, D), F32),
        pltpu.VMEM((8, D), F32),
        pltpu.VMEM((HEADS, 8, D), F32),
        pltpu.SemaphoreType.DMA((N_COPIES,)),
        pltpu.SemaphoreType.DMA((N_COPIES,)),
        pltpu.SemaphoreType.DMA((2, 2, 8)),
        pltpu.SemaphoreType.DMA((2, 2, 8)),
    ]
    scalars, vmem = pl.BlockSpec(memory_space=pltpu.SMEM), pl.BlockSpec(memory_space=pltpu.VMEM)
    return pl.pallas_call(
        main_kernel,
        out_shape=(jax.ShapeDtypeStruct(arrays[0].shape, BF16), jax.ShapeDtypeStruct(arrays[3].shape, BF16)),
        in_specs=[scalars] * 3 + [vmem] * 8,
        out_specs=(vmem, vmem),
        scratch_shapes=shapes,
        compiler_params=pltpu.CompilerParams(
            collective_id=0, has_side_effects=True, vmem_limit_bytes=VMEM_LIMIT),
        name="tiles",
    )(order, place, text_len, *arrays)


def local(video_q, video_k, video_v, text_q, text_k, text_v, q_gain, k_gain, text_len, window):
    wide = (window == 3).astype(jnp.int32)
    code = wide[:, 0] * 4 + wide[:, 1] * 2 + wide[:, 2]
    rank = jnp.zeros_like(code)
    for value, place in enumerate(RANK_OF_CODE):
        rank = jnp.where(code == value, place, rank)
    key = rank * HEADS + jnp.arange(HEADS, dtype=jnp.int32)
    position = jnp.sum((key[None, :] < key[:, None]).astype(jnp.int32), axis=1)
    places = jnp.arange(HEADS, dtype=jnp.int32)
    order = jnp.sum(jnp.where(position[None, :] == places[:, None], places[None, :], 0), axis=1)

    return main_call(order, position, text_len, (
        video_q, video_k, video_v, text_q, text_k, text_v, q_gain[None], k_gain[None]))


def solution(mesh):
    tiles, rows = P("ta", "sa", None, None), P(("ta", "sa"), None)
    return jax.shard_map(
        local, mesh=mesh,
        in_specs=(tiles, tiles, tiles, rows, rows, rows, P(), P(), P(), P()),
        out_specs=(tiles, rows),
        check_vma=False,
    )
```
